32 devices in a mesh: req: 8 (over y, x, core), tp: 4 (over z).
Axes of the slice: x: 2, y: 2, z: 4, core: 2. Of those that a mesh axis runs over, the one named last changes fastest.
Arguments:
- stream: bfloat16 [16, 64, 3584], P('req'), may hold values from -40 to 40
- queries: bfloat16 [16, 64, 3584], P('req', None, 'tp'), may hold values from -4 to 4
- key_new: bfloat16 [16, 64, 3584], P('req', None, 'tp'), may hold values from -18 to 18
- value_new: bfloat16 [16, 64, 3584], P('req', None, 'tp'), may hold values from -6 to 6
- cache_key: bfloat16 [16, 1024, 3584], P('req', None, 'tp'), may hold values from -5 to 5
- cache_value: bfloat16 [16, 1024, 3584], P('req', None, 'tp'), may hold values from -6 to 6
- cache_length: int32 [16], P('req'), may hold values from 64 to 1024, as said below
- parents: int32 [16, 64], P('req'), may hold values from -1 to 62, as said below
- accept: int32 [16, 8, 64], P('req'), may hold values from 0 to 1, as said below
- out_weight: bfloat16 [3584, 3584], P('tp'), may hold values from -0.75 to 0.75
- norm_gain: float32 [3584], replicated, may hold values from 0.1 to 1.9
- head_weight: bfloat16 [32000, 3584], P('req'), may hold values from -1 to 1
- candidate: int32 [16, 64], replicated, may hold values from 0 to 31999
- dealing: int32 [16], replicated, may hold values from 0 to 15, each once
Outputs:
- target_logprob: float32 [16, 64], P('req')
- accepted_state: bfloat16 [16, 8, 3584], P('req', None, 'tp')
The draws below stay inside these ranges and needn't reach their ends.
Inputs may be any that keep to these rules, and one draw needn't show every extreme that they name: `cache_length`: every cache holds at least 64 live positions; in every draw some slot's cache is full. `parents`: node 0 is the root with parent -1; node t > 0 lies at depth (t - 1) // 9 + 1 and its parent lies one depth above it. `accept`: row a of a slot's matrix is one-hot on the node at depth a of the accepted path, which runs from the root down the slot's tree to some node; rows past the path's end are zero; in every draw some path ends at the deepest level.
All inputs are finite; a program needn't handle non-finite values.
Results may differ from the reference program's by a relative error of at most 0.012.
Values may be sent and summed in bfloat16 or wider, within the bound.
A program may use at most 192 MiB of HBM per device.

```python
import math
import jax
import jax.numpy as jnp
import numpy as np
from jax import lax

D = 3584
HEADS = 16
HD = 224
VOCAB = 32000
CACHE = 1024
TREE = 64
ACC = 8
REQS = 16
QW = 3584


def feature_scale():
    return 0.1 * jnp.power(10.0, jnp.arange(D, dtype=jnp.float32) / D)


def draw_stream(key, part):
    row_scale = jnp.power(10.0, jax.random.uniform(jax.random.fold_in(key, 31), (REQS, TREE, 1), jnp.float32))
    values_base = jnp.clip(jax.random.normal(jax.random.fold_in(key, 32), (REQS, TREE, D), jnp.float32), -4.0, 4.0)
    return (values_base * row_scale * feature_scale()[None, None, :]).astype(jnp.bfloat16)


def draw_queries(key, part):
    values_base = jnp.clip(jax.random.normal(jax.random.fold_in(key, 42), (REQS, TREE, HEADS * HD), jnp.float32), -4.0, 4.0)
    return values_base.astype(jnp.bfloat16)


def draw_cache_key(key, part):
    values_base = jnp.clip(jax.random.normal(jax.random.fold_in(key, 43), (REQS, CACHE, HEADS * HD), jnp.float32), -4.0, 4.0)
    return values_base.astype(jnp.bfloat16)


def draw_head_weight(key, part):
    level = 3.0 / D ** 0.5
    values_base = jnp.clip(jax.random.normal(jax.random.fold_in(key, 44), (VOCAB, D), jnp.float32), -5.0, 5.0) * level
    return values_base.astype(jnp.bfloat16)


def draw_cache_length(key, part):
    halving = jax.random.randint(jax.random.fold_in(key, 51), (REQS,), 0, 4)
    trimmed = jax.random.randint(jax.random.fold_in(key, 52), (REQS,), 0, CACHE // 8)
    lengths = jnp.maximum(CACHE // jnp.left_shift(1, halving) - trimmed, TREE)
    full_slot = jax.random.randint(jax.random.fold_in(key, 53), (), 0, REQS)
    return jnp.where(jnp.arange(REQS) == full_slot, CACHE, lengths).astype(jnp.int32)


def tree_layout(key):
    node_ids = jnp.arange(TREE, dtype=jnp.int32)
    per_level = (TREE - 1) // (ACC - 1)
    depth = jnp.where(node_ids == 0, 0, (node_ids - 1) // per_level + 1)
    picks = jax.random.randint(jax.random.fold_in(key, 61), (REQS, TREE), 0, per_level)
    parents = jnp.where(depth == 0, -1, jnp.where(depth == 1, 0, 1 + (depth - 2) * per_level + picks))
    target = jax.random.randint(jax.random.fold_in(key, 62), (REQS,), 0, TREE)
    forced = jax.random.randint(jax.random.fold_in(key, 63), (), 0, REQS)
    target = jnp.where(jnp.arange(REQS) == forced, TREE - 1, target).astype(jnp.int32)
    chain_list = [target]
    current = target
    for hop_index in range(ACC - 1):
        current = jnp.maximum(jnp.take_along_axis(parents, current[:, None], axis=1)[:, 0], 0).astype(jnp.int32)
        chain_list.append(current)
    chain = jnp.stack(chain_list, axis=1)
    target_depth = depth[target]
    offsets = target_depth[:, None] - jnp.arange(ACC, dtype=jnp.int32)[None, :]
    node_at = jnp.take_along_axis(chain, jnp.clip(offsets, 0, ACC - 1), axis=1)
    hits = (node_at[:, :, None] == node_ids[None, None, :]) & (offsets >= 0)[:, :, None]
    return (parents.astype(jnp.int32), hits.astype(jnp.int32))


def draw_parents(key, part):
    return tree_layout(jax.random.fold_in(key, 60))[0]


def draw_accept(key, part):
    return tree_layout(jax.random.fold_in(key, 60))[1]


def plant(values, stream_key, low, largest):
    shape = values.shape
    place = [jax.random.randint(jax.random.fold_in(stream_key, axis), (), 0, shape[axis]) for axis in range(len(shape))]
    values = values.at[tuple(place)].set(low)
    longest = shape.index(max(shape))
    place[longest] = (place[longest] + 1) % shape[longest]
    return values.at[tuple(place)].set(largest)


def block_scale(key, shape, cuts, smallest, high):
    def one(position, shards_of):
        draws = jax.random.uniform(jax.random.fold_in(jax.random.fold_in(key, 6), position), (shards_of,), jnp.float32, smallest / len(cuts), high / len(cuts))
        return jnp.repeat(jnp.exp(draws), shape[position] // shards_of).reshape((-1,) + (1,) * (len(shape) - position - 1))

    factor_of = one(*cuts[0])
    for cut in cuts[1:]:
        factor_of = factor_of * one(*cut)
    return factor_of


def rank_bounds(count, slope):
    portions = [(1 << 20) // math.isqrt(rank ** slope) + 1 for rank in range(1, count + 1)]
    width = 1 + sum(portions) // (1 << 30)
    return np.cumsum(np.array([max(1, weight // width) for weight in portions]))


def ranked_ids(own_key, dims, count, slope):
    listing = rank_bounds(count, slope)
    lot = jax.random.randint(jax.random.fold_in(own_key, 1), dims, 0, int(listing[count - 1]))
    grade = jnp.searchsorted(jnp.asarray(listing, jnp.int32), lot, side="right")
    return jax.random.permutation(jax.random.fold_in(own_key, 2), count)[grade].astype(jnp.int32)


def noise(key, dims, spread, bound, shards=(), kind=jnp.bfloat16):
    gain = block_scale(key, dims, shards, -0.22, 0.18) if shards else 1.0
    drawn = jax.random.normal(key, dims, jnp.float32) * spread * gain
    return jnp.minimum(jnp.maximum(drawn, -bound), bound).astype(kind)


def setup_inputs(seed: int = 0) -> dict:
    keys = jax.random.split(jax.random.key(seed), 15)
    stream = draw_stream(jax.random.fold_in(keys[14], 71), 0)
    queries = draw_queries(jax.random.fold_in(keys[14], 71), 0)
    key_new = noise(keys[2], (REQS, TREE, QW), 3.0, 18.0, ((0, 8), (2, 4)))
    value_new = noise(keys[3], (REQS, TREE, QW), 1.0, 6.0, ((0, 8), (2, 4)))
    cache_key = draw_cache_key(jax.random.fold_in(keys[14], 71), 0)
    cache_value = noise(keys[5], (REQS, CACHE, QW), 1.0, 6.0, ((0, 8), (2, 4)))
    cache_length = draw_cache_length(jax.random.fold_in(keys[14], 71), 0)
    parents = draw_parents(jax.random.fold_in(keys[14], 71), 0)
    accept = draw_accept(jax.random.fold_in(keys[14], 71), 0)
    out_weight = noise(keys[9], (QW, D), (HEADS * HD // 64) ** -0.5, 0.75, ((0, 4),))
    norm_gain = jnp.clip(1.0 + 0.18 * jax.random.normal(keys[10], (D,), jnp.float32), 0.1, 1.9)
    head_weight = draw_head_weight(jax.random.fold_in(keys[14], 71), 0)
    candidate = plant(ranked_ids(keys[12], (REQS, TREE), VOCAB, 2), jax.random.fold_in(keys[12], 3), 0, VOCAB - 1).astype(jnp.int32)
    dealing = jax.random.permutation(keys[13], REQS).astype(jnp.int32)
    return dict(stream=stream, queries=queries, key_new=key_new, value_new=value_new, cache_key=cache_key, cache_value=cache_value, cache_length=cache_length, parents=parents, accept=accept, out_weight=out_weight, norm_gain=norm_gain, head_weight=head_weight, candidate=candidate, dealing=dealing)


EPS = 1e-05
HIGH = lax.Precision.HIGHEST

def ancestry(parents):
    node_count = parents.shape[-1]
    node_ids = jnp.arange(node_count, dtype=jnp.int32)
    stride_map = (parents[..., :, None] == node_ids).astype(jnp.float32)
    reached = jnp.broadcast_to(jnp.eye(node_count, dtype=jnp.float32), stride_map.shape)
    for doubling in range((ACC - 1).bit_length()):
        reached = reached + jnp.einsum('rtk,rku->rtu', reached, stride_map, precision=HIGH)
        stride_map = jnp.einsum('rtk,rku->rtu', stride_map, stride_map, precision=HIGH)
    return reached > 0.5

def rounded_weights(values):
    return lax.optimization_barrier(values.astype(jnp.bfloat16)).astype(jnp.float32)

def reference(stream, queries, key_new, value_new, cache_key, cache_value, cache_length, parents, accept, out_weight, norm_gain, head_weight, candidate, dealing):
    visible = ancestry(parents)
    factor = HD ** (-0.5)

    def attend(members):
        query_rows, tree_keys, tree_values, past_keys, past_values, live_count, seen = members
        query_rows = query_rows.astype(jnp.float32).reshape(TREE, HEADS, HD)
        past_keys = past_keys.astype(jnp.float32).reshape(CACHE, HEADS, HD)
        past_values = past_values.astype(jnp.float32).reshape(CACHE, HEADS, HD)
        tree_keys = tree_keys.astype(jnp.float32).reshape(TREE, HEADS, HD)
        tree_values = tree_values.astype(jnp.float32).reshape(TREE, HEADS, HD)
        positions = jnp.arange(CACHE, dtype=jnp.int32)
        past_scores = jnp.einsum('thd,khd->htk', query_rows, past_keys) * factor
        past_scores = jnp.where((positions < live_count)[None, None, :], past_scores, -jnp.inf)
        tree_scores = jnp.einsum('thd,khd->htk', query_rows, tree_keys) * factor
        tree_scores = jnp.where(seen[None], tree_scores, -jnp.inf)
        highest = jnp.maximum(lax.optimization_barrier(jnp.max(past_scores, axis=2)), lax.optimization_barrier(jnp.max(tree_scores, axis=2)))
        past_weights = jnp.exp(past_scores - highest[..., None])
        tree_weights = jnp.exp(tree_scores - highest[..., None])
        denominator = lax.optimization_barrier(jnp.sum(past_weights, axis=2)) + lax.optimization_barrier(jnp.sum(tree_weights, axis=2))
        mixed = jnp.einsum('htk,khd->htd', rounded_weights(past_weights), past_values)
        mixed = mixed + jnp.einsum('htk,khd->htd', rounded_weights(tree_weights), tree_values)
        mixed = mixed / denominator[..., None]
        return mixed.transpose(1, 0, 2).reshape(TREE, HEADS * HD).astype(jnp.bfloat16)
    attention = lax.map(attend, (queries, key_new, value_new, cache_key, cache_value, cache_length, visible))
    projected = jnp.dot(attention.reshape(REQS * TREE, HEADS * HD), out_weight, preferred_element_type=jnp.float32)
    post_rows = (stream.reshape(REQS * TREE, D).astype(jnp.float32) + projected).astype(jnp.bfloat16)
    post_float = post_rows.astype(jnp.float32)
    inverse = lax.rsqrt(lax.optimization_barrier(jnp.mean(post_float * post_float, axis=1, keepdims=True)) + EPS)
    normed = (post_float * inverse * norm_gain.astype(jnp.float32)[None, :]).astype(jnp.bfloat16)

    def head_block(members):
        block_rows, block_ids = members
        logits = lax.dot_general(block_rows, head_weight, (((1,), (1,)), ((), ())), preferred_element_type=jnp.float32)
        highest = lax.optimization_barrier(jnp.max(logits, axis=1))
        summed = lax.optimization_barrier(jnp.sum(jnp.exp(logits - highest[:, None]), axis=1))
        words = jnp.arange(VOCAB, dtype=jnp.int32)
        picked = lax.optimization_barrier(jnp.sum(jnp.where(words[None, :] == block_ids[:, None], logits, 0.0), axis=1))
        return picked - highest - jnp.log(summed)
    block_size = 512
    slot_logprob = lax.map(head_block, (normed.reshape(-1, block_size, D), candidate.reshape(-1, block_size))).reshape(REQS, TREE)
    reorder = (dealing[None, :] == jnp.arange(REQS, dtype=jnp.int32)[:, None]).astype(jnp.float32)
    target_logprob = jnp.dot(reorder, slot_logprob, precision=HIGH)
    compact = jnp.einsum('sat,std->sad', accept.astype(jnp.float32), post_float.reshape(REQS, TREE, D), precision=HIGH)
    accepted_state = jnp.einsum('rs,sad->rad', reorder, compact, precision=HIGH).astype(jnp.bfloat16)
    return (target_logprob, accepted_state)
```

```python
import functools

import jax
import jax.numpy as jnp
from jax import lax
from jax.experimental import pallas as pl
from jax.experimental.pallas import tpu as pltpu
from jax.sharding import PartitionSpec as P

HD = 224
ACC = 8
EPS = 1e-05
NTP = 4
MESH = pl.DeviceIdType.MESH
NT = (((1,), (1,)), ((), ()))
F32 = jnp.float32
BF16 = jnp.bfloat16


def vocab_chunk(vocab):
    for size in (400, 512, 256):
        if vocab % size == 0:
            return size
    return vocab


def kernel(
    n_req,
    len_ref,
    par_ref,
    acc_ref,
    gain_ref,
    want_ref,
    q_hbm,
    kn_hbm,
    vn_hbm,
    stream_hbm,
    ck_hbm,
    cv_hbm,
    ow_hbm,
    hw_hbm,
    lp_out,
    acc_out,
    q_v,
    kn_v,
    vn_v,
    st_v,
    ck_v,
    cv_v,
    ow_v,
    hw_v,
    part,
    zrecv,
    zfwd,
    gat,
    post_v,
    acc_part,
    acc_recv,
    acc_all,
    stats,
    lpz,
    in_sem,
    hw_sem,
    zs_sem,
    zr_sem,
    gs_sem,
    gf_sem,
    gr_sem,
    as_sem,
    ar_sem,
    bs_sem,
    br_sem,
    ss_sem,
    sr_sem,
    ls_sem,
    lr_sem,
):
    slots, tree, width = q_v.shape
    heads = width // HD
    model = ow_v.shape[1]
    vocab = hw_v.shape[0]
    share = tree // NTP
    rows = n_req * share
    dslice = model // NTP
    chips = n_req // 2
    r = lax.axis_index("req")
    z = lax.axis_index("tp")
    chip = r // 2
    core = r % 2
    sibling = chip * 2 + (1 - core)

    def near(step):
        return lax.rem(r + step, n_req), z

    def along(step):
        return r, lax.rem(z + step, NTP)

    loads = {}

    def load(name, index, src, dst):
        loads[name] = pltpu.make_async_copy(src, dst, in_sem.at[index])
        loads[name].start()

    load("q", 0, q_hbm, q_v)
    load("k0", 1, ck_hbm.at[0], ck_v.at[0])
    load("kn", 2, kn_hbm, kn_v)
    load("vn", 3, vn_hbm, vn_v)
    load("v0", 4, cv_hbm.at[0], cv_v.at[0])
    load("ow", 5, ow_hbm, ow_v)
    load("k1", 6, ck_hbm.at[1], ck_v.at[1])
    load("v1", 7, cv_hbm.at[1], cv_v.at[1])
    own_rows = pl.ds(pl.multiple_of(z * share, share), share)
    load("st", 8, stream_hbm.at[:, own_rows, :], st_v)
    chunk = vocab_chunk(vocab)
    n_chunks = vocab // chunk
    head_loads = []
    for c in range(n_chunks):
        rows_c = pl.ds(c * chunk, chunk)
        copy = pltpu.make_async_copy(hw_hbm.at[rows_c, :], hw_v.at[rows_c, :], hw_sem.at[c])
        copy.start()
        head_loads.append(copy)

    barrier = pltpu.get_barrier_semaphore()
    for step in range(1, n_req):
        pl.semaphore_signal(barrier, inc=1, device_id=near(step), device_id_type=MESH)
    for step in range(1, NTP):
        pl.semaphore_signal(barrier, inc=1, device_id=along(step), device_id_type=MESH)

    def remote(src, dst, send, recv, device):
        return pltpu.make_async_remote_copy(
            src_ref=src, dst_ref=dst, send_sem=send, recv_sem=recv, device_id=device, device_id_type=MESH
        )

    row_id = lax.broadcasted_iota(jnp.int32, (tree, tree), 0)
    col_id = lax.broadcasted_iota(jnp.int32, (tree, tree), 1)
    eye = (row_id == col_id).astype(F32)
    visible = []
    for s in range(slots):
        step_t = (row_id == par_ref[s : s + 1, :]).astype(F32).astype(BF16)
        reached = eye
        for doubling in range((ACC - 1).bit_length()):
            reached = reached + lax.dot_general(reached.astype(BF16), step_t, NT, preferred_element_type=F32)
            step_t = jnp.dot(step_t, step_t, preferred_element_type=F32).astype(BF16)
        visible.append(reached)

    lane = lax.broadcasted_iota(jnp.int32, (tree, width), 1)
    head_mask = [(lane >= h * HD) & (lane < (h + 1) * HD) for h in range(heads)]
    scale = HD ** (-0.5)

    def attend(s):
        query = q_v[s]
        blocks = jnp.concatenate([jnp.where(m, query, jnp.zeros_like(query)) for m in head_mask], axis=0)
        past = lax.dot_general(blocks, ck_v[s], NT, preferred_element_type=F32) * scale
        fresh = lax.dot_general(blocks, kn_v[s], NT, preferred_element_type=F32) * scale
        position = lax.broadcasted_iota(jnp.int32, past.shape, 1)
        past = jnp.where(position < len_ref[s], past, -jnp.inf)
        seen = jnp.concatenate([visible[s]] * heads, axis=0)
        fresh = jnp.where(seen > 0.5, fresh, -jnp.inf)
        top = jnp.maximum(jnp.max(past, axis=1, keepdims=True), jnp.max(fresh, axis=1, keepdims=True))
        past = jnp.exp(past - top)
        fresh = jnp.exp(fresh - top)
        total = jnp.sum(past, axis=1, keepdims=True) + jnp.sum(fresh, axis=1, keepdims=True)
        if s == 0:
            loads["v0"].wait()
        else:
            loads["v1"].wait()
        mixed = jnp.dot(past.astype(BF16), cv_v[s], preferred_element_type=F32)
        mixed = mixed + jnp.dot(fresh.astype(BF16), vn_v[s], preferred_element_type=F32)
        mixed = mixed / total
        joined = jnp.zeros((tree, width), F32)
        for h in range(heads):
            joined = jnp.where(head_mask[h], mixed[h * tree : (h + 1) * tree, :], joined)
        return joined.astype(BF16)

    low = z < 2
    edge = (z == 0) | (z == 3)
    mate = z + 1 - 2 * (z % 2)
    far_edge = jnp.where(low, 3, 0)
    far_inner = jnp.where(low, 2, 1)

    def block(index):
        return pl.ds(pl.multiple_of(index * share, share), share)

    far_slot = jnp.where(edge, 2, 1)
    far_copy = [
        remote(
            part.at[s, block(far_edge), :], zrecv.at[s, far_slot], zs_sem.at[s, 0], zr_sem.at[s, far_slot], (r, far_edge)
        )
        for s in range(slots)
    ]
    mate_copy = [
        remote(part.at[s, block(mate), :], zrecv.at[s, 0], zs_sem.at[s, 1], zr_sem.at[s, 0], (r, mate))
        for s in range(slots)
    ]
    edge_copy = [
        remote(part.at[s, block(far_inner), :], zrecv.at[s, 2], zs_sem.at[s, 2], zr_sem.at[s, 2], (r, mate))
        for s in range(slots)
    ]
    sum_copy = [
        remote(zfwd.at[s], zrecv.at[s, 1], zs_sem.at[s, 2], zr_sem.at[s, 1], (r, far_inner)) for s in range(slots)
    ]

    def landed(s, slot):
        remote(zfwd.at[s], zrecv.at[s, slot], zs_sem.at[s, 0], zr_sem.at[s, slot], (r, mate)).wait_recv()

    loads["q"].wait()
    for s in range(slots):
        loads["k0" if s == 0 else "k1"].wait()
        if s == 0:
            loads["kn"].wait()
            loads["vn"].wait()
        attention = attend(s)
        if s == 0:
            loads["ow"].wait()

        def project(step, carry, s=s, attention=attention):
            columns = pl.ds(pl.multiple_of(step * 512, 512), 512)
            part[s, :, columns] = jnp.dot(attention, ow_v[:, columns], preferred_element_type=F32).astype(BF16)
            return carry

        lax.fori_loop(0, model // 512, project, 0)
        if s == 0:
            pl.semaphore_wait(barrier, n_req - 1 + NTP - 1)

        @pl.when(edge)
        def _(s=s):
            edge_copy[s].start()

        far_copy[s].start()
        mate_copy[s].start()

    loads["st"].wait()

    def forward_sum(s):
        @pl.when(jnp.logical_not(edge))
        def _():
            landed(s, 2)
            zfwd[s] = (part[s, block(far_inner), :].astype(F32) + zrecv[s, 2].astype(F32)).astype(BF16)
            sum_copy[s].start()

    gather_peers = [lax.rem(chip + step, chips) * 2 + core for step in range(1, chips)]
    gather_sources = [lax.rem(chip + chips - step, chips) * 2 + core for step in range(1, chips)]

    def gather_copy(s, owner, send, device):
        return remote(gat.at[s, owner], gat.at[s, owner], send, gr_sem.at[s, owner], (device, z))

    def finish(s):
        landed(s, 0)
        landed(s, 1)

        @pl.when(edge)
        def _():
            landed(s, 2)

        total = part[s, own_rows, :].astype(F32) + zrecv[s, 0].astype(F32) + zrecv[s, 1].astype(F32)
        third = jnp.where(edge, zrecv[s, 2].astype(F32), 0.0)
        post = (st_v[s].astype(F32) + (total + third)).astype(BF16)
        post_v[s] = post
        post = post.astype(F32)
        inverse = lax.rsqrt(jnp.mean(post * post, axis=1, keepdims=True) + EPS)
        gat[s, r] = (post * inverse * gain_ref[...]).astype(BF16)
        for step in range(1, chips):
            gather_copy(s, r, gs_sem.at[s, step], gather_peers[step - 1]).start()
        gather_copy(s, r, gs_sem.at[s, 0], sibling).start()

    def forward_gather(s):
        for step in range(1, chips):
            source = gather_sources[step - 1]
            gather_copy(s, source, gf_sem.at[s, step], sibling).wait_recv()
            gather_copy(s, source, gf_sem.at[s, step], sibling).start()

    forward_sum(0)
    finish(0)
    forward_sum(1)
    forward_gather(0)
    finish(1)

    node = lax.broadcasted_iota(jnp.int32, (tree, share), 0)
    place = lax.broadcasted_iota(jnp.int32, (tree, share), 1)
    pick = (node == place + z * share).astype(F32).astype(BF16)
    for s in range(slots):
        chosen = jnp.dot(acc_ref[s].astype(F32).astype(BF16), pick, preferred_element_type=F32).astype(BF16)
        for k in range(NTP):
            acc_part[k, s] = jnp.dot(
                chosen, post_v[s, :, k * dslice : (k + 1) * dslice], preferred_element_type=F32
            )
    acc_send = []
    for k in range(NTP):
        acc_recv[NTP + 1 + k] = jnp.concatenate([acc_part[k, s] for s in range(slots)], axis=0).astype(BF16)
    for step in range(1, NTP):
        target = lax.rem(z + step, NTP)
        copy = remote(
            acc_recv.at[NTP + 1 + target], acc_recv.at[step], as_sem.at[step], ar_sem.at[step], (r, target)
        )
        copy.start()
        acc_send.append(copy)

    forward_gather(1)

    for copy in acc_send:
        copy.wait_recv()
    compact = acc_recv[NTP + 1 + z].astype(F32)
    for step in range(1, NTP):
        compact = compact + acc_recv[step].astype(F32)
    acc_all[r] = compact.astype(BF16)
    acc_copies = []
    for step in range(1, n_req):
        copy = remote(acc_all.at[r], acc_all.at[r], bs_sem.at[step], br_sem.at[r], near(step))
        copy.start()
        acc_copies.append(copy)

    for s in range(slots):
        gather_copy(s, sibling, gs_sem.at[s, 0], sibling).wait_recv()
        for step in range(1, chips):
            other = lax.rem(chip + step, chips) * 2 + (1 - core)
            gather_copy(s, other, gs_sem.at[s, 0], sibling).wait_recv()
    for copy in head_loads:
        copy.wait()

    everyone = jnp.concatenate([gat[s].reshape(rows, model) for s in range(slots)], axis=0)
    wanted = want_ref[...] - r * vocab
    count = slots * rows

    def visit(c, carry):
        top, total, picked = carry
        words = hw_v[pl.ds(pl.multiple_of(c * chunk, chunk), chunk), :]
        logits = lax.dot_general(words, everyone, NT, preferred_element_type=F32)
        new_top = jnp.maximum(top, jnp.max(logits, axis=0, keepdims=True))
        total = total * jnp.exp(top - new_top) + jnp.sum(jnp.exp(logits - new_top), axis=0, keepdims=True)
        ids = lax.broadcasted_iota(jnp.int32, logits.shape, 0) + c * chunk
        picked = picked + jnp.sum(jnp.where(ids == wanted, logits, 0.0), axis=0, keepdims=True)
        return new_top, total, picked

    start = (jnp.full((1, count), -1e30, F32), jnp.zeros((1, count), F32), jnp.zeros((1, count), F32))
    top, total, picked = lax.fori_loop(0, n_chunks, visit, start)
    stats[r] = jnp.concatenate([top, total, picked, jnp.zeros((5, count), F32)], axis=0)

    stat_copies = []
    for step in range(1, n_req):
        copy = remote(stats.at[r], stats.at[r], ss_sem.at[step], sr_sem.at[r], near(step))
        copy.start()
        stat_copies.append(copy)
    for step in range(1, n_req):
        source = lax.rem(r + n_req - step, n_req)
        remote(stats.at[source], stats.at[source], ss_sem.at[step], sr_sem.at[source], near(step)).wait_recv()
    every = stats[...]
    top = jnp.max(every[:, 0, :], axis=0, keepdims=True)
    total = jnp.sum(every[:, 1, :] * jnp.exp(every[:, 0, :] - top), axis=0, keepdims=True)
    picked = jnp.sum(every[:, 2, :], axis=0, keepdims=True)
    lpz[z] = jnp.broadcast_to(picked - top - jnp.log(total), (8, count))
    lp_copies = []
    for step in range(1, NTP):
        copy = remote(lpz.at[z], lpz.at[z], ls_sem.at[step], lr_sem.at[z], along(step))
        copy.start()
        lp_copies.append(copy)
    for step in range(1, n_req):
        source = lax.rem(r + n_req - step, n_req)
        remote(acc_all.at[source], acc_all.at[source], bs_sem.at[step], br_sem.at[source], near(step)).wait_recv()
    acc_out[...] = acc_all[...]
    for step in range(1, NTP):
        source = lax.rem(z + NTP - step, NTP)
        remote(lpz.at[source], lpz.at[source], ls_sem.at[step], lr_sem.at[source], along(step)).wait_recv()
    lp_out[...] = lpz[...]

    for s in range(slots):
        far_copy[s].wait_send()
        mate_copy[s].wait_send()
        edge_copy[s].wait_send()
        for step in range(chips):
            gather_copy(s, r, gs_sem.at[s, step], sibling).wait_send()
        for step in range(1, chips):
            gather_copy(s, r, gf_sem.at[s, step], sibling).wait_send()
    for copy in acc_send + acc_copies + stat_copies + lp_copies:
        copy.wait_send()


def local(
    stream,
    queries,
    key_new,
    value_new,
    cache_key,
    cache_value,
    cache_length,
    parents,
    accept,
    out_weight,
    norm_gain,
    head_weight,
    candidate,
    dealing,
):
    slots, tree, width = queries.shape
    model = stream.shape[2]
    n_req = lax.axis_size("req")
    z = lax.axis_index("tp")
    r = lax.axis_index("req")
    share = tree // NTP
    count = slots * n_req * share
    dslice = model // NTP
    chips = n_req // 2
    vocab = head_weight.shape[0]
    cache = cache_key.shape[1]
    wanted = lax.dynamic_index_in_dim(candidate.reshape(n_req, slots, NTP, share), z, 2, keepdims=False)
    wanted = wanted.transpose(1, 0, 2).reshape(1, count)
    vmem = pl.BlockSpec(memory_space=pltpu.VMEM)
    hbm = pl.BlockSpec(memory_space=pl.ANY)
    dma = pltpu.SemaphoreType.DMA
    logprob, states = pl.pallas_call(
        functools.partial(kernel, n_req),
        out_shape=(
            jax.ShapeDtypeStruct((NTP, 8, count), F32),
            jax.ShapeDtypeStruct((n_req, slots * ACC, dslice), BF16),
        ),
        in_specs=[pl.BlockSpec(memory_space=pltpu.SMEM)] + [vmem] * 4 + [hbm] * 8,
        out_specs=(vmem, vmem),
        scratch_shapes=[
            pltpu.VMEM((slots, tree, width), BF16),
            pltpu.VMEM((slots, tree, width), BF16),
            pltpu.VMEM((slots, tree, width), BF16),
            pltpu.VMEM((slots, share, model), BF16),
            pltpu.VMEM((slots, cache, width), BF16),
            pltpu.VMEM((slots, cache, width), BF16),
            pltpu.VMEM((width, model), BF16),
            pltpu.VMEM((vocab, model), BF16),
            pltpu.VMEM((slots, tree, model), BF16),
            pltpu.VMEM((slots, 3, share, model), BF16),
            pltpu.VMEM((slots, share, model), BF16),
            pltpu.VMEM((slots, n_req, share, model), BF16),
            pltpu.VMEM((slots, share, model), BF16),
            pltpu.VMEM((NTP, slots, ACC, dslice), F32),
            pltpu.VMEM((2 * NTP + 1, slots * ACC, dslice), BF16),
            pltpu.VMEM((n_req, slots * ACC, dslice), BF16),
            pltpu.VMEM((n_req, 8, count), F32),
            pltpu.VMEM((NTP, 8, count), F32),
            dma((9,)),
            dma((vocab // vocab_chunk(vocab),)),
            dma((slots, 3)),
            dma((slots, 3)),
            dma((slots, chips)),
            dma((slots, chips)),
            dma((slots, n_req)),
            dma((NTP,)),
            dma((NTP,)),
            dma((n_req,)),
            dma((n_req,)),
            dma((n_req,)),
            dma((n_req,)),
            dma((NTP,)),
            dma((NTP,)),
        ],
        compiler_params=pltpu.CompilerParams(
            collective_id=0, has_side_effects=True, vmem_limit_bytes=62 * 1024 * 1024
        ),
    )(
        cache_length,
        parents,
        accept,
        norm_gain.reshape(1, model),
        wanted,
        queries,
        key_new,
        value_new,
        stream,
        cache_key,
        cache_value,
        out_weight,
        head_weight,
    )
    own = r * slots + jnp.arange(slots, dtype=jnp.int32)
    selector = dealing[None, :] == own[:, None]
    by_slot = logprob[:, 0, :].reshape(NTP, slots, n_req, share).transpose(2, 1, 0, 3).reshape(n_req * slots, tree)
    target_logprob = jnp.sum(jnp.where(selector[:, :, None], by_slot[None], 0.0), axis=1)
    states = states.reshape(n_req * slots, ACC, dslice).astype(F32)
    accepted_state = jnp.sum(jnp.where(selector[:, :, None, None], states[None], 0.0), axis=1).astype(BF16)
    return (target_logprob, accepted_state)


def solution(mesh):
    placed = (
        P("req", None, None),
        P("req", None, "tp"),
        P("req", None, "tp"),
        P("req", None, "tp"),
        P("req", None, "tp"),
        P("req", None, "tp"),
        P("req"),
        P("req", None),
        P("req", None, None),
        P("tp", None),
        P(),
        P("req", None),
        P(),
        P(),
    )
    return jax.shard_map(
        local,
        mesh=mesh,
        in_specs=placed,
        out_specs=(P("req", None), P("req", None, "tp")),
        check_vma=False,
    )
```

```python
import functools

import jax
import jax.numpy as jnp
from jax import lax
from jax.experimental import pallas as pl
from jax.experimental.pallas import tpu as pltpu
from jax.sharding import PartitionSpec as P

HD = 224
ACC = 8
EPS = 1e-05
NTP = 4
MESH = pl.DeviceIdType.MESH
NT = (((1,), (1,)), ((), ()))
HIGH = lax.Precision.HIGHEST
F32 = jnp.float32
BF16 = jnp.bfloat16


def feature_chunks(model):
    size = 1024
    return [(first, min(size, model - first)) for first in range(0, model, size)]


def vocab_chunk(vocab):
    for size in (800, 512, 256):
        if vocab % size == 0:
            return size
    return vocab


def kernel(
    n_req,
    len_ref,
    par_ref,
    acc_ref,
    gain_ref,
    cand_ref,
    deal_ref,
    q_hbm,
    kn_hbm,
    vn_hbm,
    stream_hbm,
    ck_hbm,
    cv_hbm,
    ow_hbm,
    hw_hbm,
    lp_out,
    acc_out,
    q_v,
    kn_v,
    vn_v,
    st_v,
    ck_v,
    cv_v,
    ow_v,
    hw_v,
    part,
    zrecv,
    zfwd,
    gat,
    post_v,
    logits_v,
    norms,
    acc_part,
    acc_recv,
    acc_all,
    stats,
    lpz,
    in_sem,
    hw_sem,
    zs_sem,
    zr_sem,
    gs_sem,
    gf_sem,
    gr_sem,
    as_sem,
    ar_sem,
    bs_sem,
    br_sem,
    ss_sem,
    sr_sem,
    ls_sem,
    lr_sem,
    ns_sem,
    nr_sem,
):
    slots, tree, width = q_v.shape
    heads = width // HD
    model = ow_v.shape[1]
    vocab = hw_v.shape[0]
    share = tree // NTP
    rows = n_req * share
    dslice = model // NTP
    chips = n_req // 2
    r = lax.axis_index("req")
    z = lax.axis_index("tp")
    chip = r // 2
    core = r % 2
    sibling = chip * 2 + (1 - core)

    def near(step):
        return lax.rem(r + step, n_req), z

    def along(step):
        return r, lax.rem(z + step, NTP)

    loads = {}

    def load(name, index, src, dst):
        loads[name] = pltpu.make_async_copy(src, dst, in_sem.at[index])
        loads[name].start()

    load("q", 0, q_hbm, q_v)
    load("k0", 1, ck_hbm.at[0], ck_v.at[0])
    load("kn", 2, kn_hbm, kn_v)
    load("vn", 3, vn_hbm, vn_v)
    load("v0", 4, cv_hbm.at[0], cv_v.at[0])
    load("ow", 5, ow_hbm, ow_v)
    load("k1", 6, ck_hbm.at[1], ck_v.at[1])
    load("v1", 7, cv_hbm.at[1], cv_v.at[1])
    own_rows = pl.ds(pl.multiple_of(z * share, share), share)
    load("st", 8, stream_hbm.at[:, own_rows, :], st_v)
    chunk = vocab_chunk(vocab)
    n_chunks = vocab // chunk
    head_loads = []
    for c in range(n_chunks):
        rows_c = pl.ds(c * chunk, chunk)
        head_loads.append(pltpu.make_async_copy(hw_hbm.at[rows_c, :], hw_v.at[rows_c, :], hw_sem.at[c]))

    barrier = pltpu.get_barrier_semaphore()
    for step in range(1, n_req):
        pl.semaphore_signal(barrier, inc=1, device_id=near(step), device_id_type=MESH)
    for step in range(1, NTP):
        pl.semaphore_signal(barrier, inc=1, device_id=along(step), device_id_type=MESH)

    def remote(src, dst, send, recv, device):
        return pltpu.make_async_remote_copy(
            src_ref=src, dst_ref=dst, send_sem=send, recv_sem=recv, device_id=device, device_id_type=MESH
        )

    row_id = lax.broadcasted_iota(jnp.int32, (tree, tree), 0)
    col_id = lax.broadcasted_iota(jnp.int32, (tree, tree), 1)
    eye = (row_id == col_id).astype(F32)
    visible = []
    for s in range(slots):
        step_t = (row_id == par_ref[s : s + 1, :]).astype(F32).astype(BF16)
        reached = eye
        for doubling in range((ACC - 1).bit_length()):
            reached = reached + lax.dot_general(reached.astype(BF16), step_t, NT, preferred_element_type=F32)
            step_t = jnp.dot(step_t, step_t, preferred_element_type=F32).astype(BF16)
        visible.append(reached)

    lane = lax.broadcasted_iota(jnp.int32, (tree, width), 1)
    head_mask = [(lane >= h * HD) & (lane < (h + 1) * HD) for h in range(heads)]
    scale = HD ** (-0.5)

    def attend(s):
        query = q_v[s]
        blocks = jnp.concatenate([jnp.where(m, query, jnp.zeros_like(query)) for m in head_mask], axis=0)
        past = lax.dot_general(blocks, ck_v[s], NT, preferred_element_type=F32) * scale
        fresh = lax.dot_general(blocks, kn_v[s], NT, preferred_element_type=F32) * scale
        position = lax.broadcasted_iota(jnp.int32, past.shape, 1)
        past = jnp.where(position < len_ref[s], past, -jnp.inf)
        seen = jnp.concatenate([visible[s]] * heads, axis=0)
        fresh = jnp.where(seen > 0.5, fresh, -jnp.inf)
        top = jnp.maximum(jnp.max(past, axis=1, keepdims=True), jnp.max(fresh, axis=1, keepdims=True))
        past = jnp.exp(past - top)
        fresh = jnp.exp(fresh - top)
        total = jnp.sum(past, axis=1, keepdims=True) + jnp.sum(fresh, axis=1, keepdims=True)
        if s == 0:
            loads["v0"].wait()
        else:
            loads["v1"].wait()
        mixed = jnp.dot(past.astype(BF16), cv_v[s], preferred_element_type=F32)
        mixed = mixed + jnp.dot(fresh.astype(BF16), vn_v[s], preferred_element_type=F32)
        mixed = mixed / total
        joined = jnp.zeros((tree, width), F32)
        for h in range(heads):
            joined = jnp.where(head_mask[h], mixed[h * tree : (h + 1) * tree, :], joined)
        return joined.astype(BF16)

    low = z < 2
    edge = (z == 0) | (z == 3)
    mate = z + 1 - 2 * (z % 2)
    far_edge = jnp.where(low, 3, 0)
    far_inner = jnp.where(low, 2, 1)

    def block(index):
        return pl.ds(pl.multiple_of(index * share, share), share)

    far_slot = jnp.where(edge, 2, 1)
    chunks = feature_chunks(model)
    n_feat = len(chunks)
    stages = [(s, f) for s in range(slots) for f in range(n_feat)]
    spans = [pl.ds(first, size) for first, size in chunks]

    def z_copy(s, f, src, slot, lane_sem, device):
        dst = zrecv.at[s, slot, :, spans[f]]
        return remote(src, dst, zs_sem.at[s, f, lane_sem], zr_sem.at[s, f, slot], (r, device))

    def far_copy(s, f):
        return z_copy(s, f, part.at[s, block(far_edge), spans[f]], far_slot, 0, far_edge)

    def mate_copy(s, f):
        return z_copy(s, f, part.at[s, block(mate), spans[f]], 0, 1, mate)

    def edge_copy(s, f):
        return z_copy(s, f, part.at[s, block(far_inner), spans[f]], 2, 2, mate)

    def sum_copy(s, f):
        return z_copy(s, f, zfwd.at[s, :, spans[f]], 1, 2, far_inner)

    def landed(s, f, slot):
        z_copy(s, f, zfwd.at[s, :, spans[f]], slot, 0, mate).wait_recv()

    loads["q"].wait()
    for s in range(slots):
        loads["k0" if s == 0 else "k1"].wait()
        if s == 0:
            loads["kn"].wait()
            loads["vn"].wait()
        attention = attend(s)
        if s == 0:
            loads["ow"].wait()
            for copy in head_loads:
                copy.start()
            pl.semaphore_wait(barrier, n_req - 1 + NTP - 1)
        for f in range(n_feat):
            part[s, :, spans[f]] = jnp.dot(
                attention, ow_v[:, spans[f]], preferred_element_type=F32
            ).astype(BF16)

            @pl.when(edge)
            def _(s=s, f=f):
                edge_copy(s, f).start()

            far_copy(s, f).start()
            mate_copy(s, f).start()

    loads["st"].wait()

    def forward_sum(s, f):
        @pl.when(jnp.logical_not(edge))
        def _():
            landed(s, f, 2)
            own = part[s, block(far_inner), spans[f]].astype(F32)
            zfwd[s, :, spans[f]] = (own + zrecv[s, 2, :, spans[f]].astype(F32)).astype(BF16)
            sum_copy(s, f).start()

    gather_peers = [lax.rem(chip + step, chips) * 2 + core for step in range(1, chips)]
    gather_sources = [lax.rem(chip + chips - step, chips) * 2 + core for step in range(1, chips)]

    def gather_copy(s, f, owner, send, device):
        place = gat.at[s, owner, :, spans[f]]
        return remote(place, place, send, gr_sem.at[s, f, owner], (device, z))

    squares = [jnp.zeros((share, 1), F32) for s in range(slots)]

    def finish(s, f):
        landed(s, f, 0)
        landed(s, f, 1)

        @pl.when(edge)
        def _():
            landed(s, f, 2)

        span = spans[f]
        total = part[s, own_rows, span].astype(F32) + zrecv[s, 0, :, span].astype(F32)
        total = total + zrecv[s, 1, :, span].astype(F32)
        third = jnp.where(edge, zrecv[s, 2, :, span].astype(F32), 0.0)
        post = (st_v[s, :, span].astype(F32) + (total + third)).astype(BF16)
        post_v[s, :, span] = post
        post = post.astype(F32)
        squares[s] = squares[s] + jnp.sum(post * post, axis=1, keepdims=True)
        gat[s, r, :, span] = (post * gain_ref[span].reshape(1, chunks[f][1])).astype(BF16)
        for step in range(1, chips):
            gather_copy(s, f, r, gs_sem.at[s, f, step], gather_peers[step - 1]).start()
        gather_copy(s, f, r, gs_sem.at[s, f, 0], sibling).start()

    def forward_gather(s, f):
        for step in range(1, chips):
            source = gather_sources[step - 1]
            gather_copy(s, f, source, gf_sem.at[s, f, step], sibling).wait_recv()
            gather_copy(s, f, source, gf_sem.at[s, f, step], sibling).start()

    def gathered(s, f):
        gather_copy(s, f, sibling, gs_sem.at[s, f, 0], sibling).wait_recv()
        for step in range(1, chips):
            other = lax.rem(chip + step, chips) * 2 + (1 - core)
            gather_copy(s, f, other, gs_sem.at[s, f, 0], sibling).wait_recv()

    count = slots * rows

    def words_at(c):
        return pl.ds(pl.multiple_of(c * chunk, chunk), chunk)

    def head_part(f, c):
        inputs = gat[:, :, :, spans[f]].reshape(count, chunks[f][1])
        return lax.dot_general(hw_v[words_at(c), spans[f]], inputs, NT, preferred_element_type=F32)

    def score(f):
        for s in range(slots):
            gathered(s, f)
        if f == 0:
            for copy in head_loads:
                copy.wait()
        if f < n_feat - 1:

            def visit(c, carry):
                if f == 0:
                    logits_v[words_at(c), :] = head_part(f, c)
                else:
                    logits_v[words_at(c), :] += head_part(f, c)
                return carry

            lax.fori_loop(0, n_chunks, visit, 0)

    lane_id = lax.broadcasted_iota(jnp.int32, (1, count), 1)
    lane_slot = lax.rem(lane_id // share, n_req) * slots + lane_id // rows
    lane_node = lax.rem(lane_id, share)

    forward_sum(*stages[0])
    n_stage = len(stages)
    norm_copies = []
    for k in range(n_stage):
        if k + 1 < n_stage:
            forward_sum(*stages[k + 1])
        finish(*stages[k])
        if k == n_stage - 1:
            own_lane = [
                lax.broadcasted_iota(jnp.int32, (share, count), 1)
                == lax.broadcasted_iota(jnp.int32, (share, count), 0) + (s * rows + r * share)
                for s in range(slots)
            ]
            placed = sum(
                jnp.sum(jnp.where(own_lane[s], lax.rsqrt(squares[s] / model + EPS), 0.0), axis=0, keepdims=True)
                for s in range(slots)
            )
            norms[r] = jnp.broadcast_to(placed, (8, count))
            for step in range(1, n_req):
                copy = remote(norms.at[r], norms.at[r], ns_sem.at[step], nr_sem.at[r], near(step))
                copy.start()
                norm_copies.append(copy)
        if k >= 1:
            forward_gather(*stages[k - 1])
        if k >= n_feat + 2:
            score(k - n_feat - 2)
    forward_gather(*stages[n_stage - 1])

    node = lax.broadcasted_iota(jnp.int32, (tree, share), 0)
    place = lax.broadcasted_iota(jnp.int32, (tree, share), 1)
    pick = (node == place + z * share).astype(F32).astype(BF16)
    for s in range(slots):
        chosen = jnp.dot(acc_ref[s].astype(F32).astype(BF16), pick, preferred_element_type=F32).astype(BF16)
        for k in range(NTP):
            acc_part[k, s] = jnp.dot(
                chosen, post_v[s, :, k * dslice : (k + 1) * dslice], preferred_element_type=F32
            )
    acc_send = []
    for k in range(NTP):
        acc_recv[NTP + 1 + k] = jnp.concatenate([acc_part[k, s] for s in range(slots)], axis=0).astype(BF16)
    for step in range(1, NTP):
        target = lax.rem(z + step, NTP)
        copy = remote(
            acc_recv.at[NTP + 1 + target], acc_recv.at[step], as_sem.at[step], ar_sem.at[step], (r, target)
        )
        copy.start()
        acc_send.append(copy)

    for f in range(max(n_feat - 2, 0), n_feat - 1):
        score(f)

    for copy in acc_send:
        copy.wait_recv()
    compact = acc_recv[NTP + 1 + z].astype(F32)
    for step in range(1, NTP):
        compact = compact + acc_recv[step].astype(F32)
    acc_all[r] = compact.astype(BF16)
    acc_copies = []
    for step in range(1, n_req):
        copy = remote(acc_all.at[r], acc_all.at[r], bs_sem.at[step], br_sem.at[r], near(step))
        copy.start()
        acc_copies.append(copy)

    wide = lax.broadcasted_iota(jnp.int32, (tree, count), 0)
    spread = (wide == lane_node + z * share).astype(F32)
    ids_by_slot = jnp.dot(cand_ref[...].astype(F32), spread, precision=HIGH, preferred_element_type=F32)
    slot_row = lax.broadcasted_iota(jnp.int32, ids_by_slot.shape, 0)
    wanted = jnp.sum(jnp.where(slot_row == lane_slot, ids_by_slot, 0.0), axis=0, keepdims=True)
    wanted = (wanted + 0.5).astype(jnp.int32) - r * vocab

    score(n_feat - 1)
    for step in range(1, n_req):
        source = lax.rem(r + n_req - step, n_req)
        remote(norms.at[source], norms.at[source], ns_sem.at[step], nr_sem.at[source], near(step)).wait_recv()
    inverse = jnp.sum(norms[:, 0, :], axis=0, keepdims=True)

    def visit(c, carry):
        top, total, picked = carry
        logits = head_part(n_feat - 1, c)
        if n_feat > 1:
            logits = logits + logits_v[words_at(c), :]
        logits = logits * inverse
        new_top = jnp.maximum(top, jnp.max(logits, axis=0, keepdims=True))
        total = total * jnp.exp(top - new_top) + jnp.sum(jnp.exp(logits - new_top), axis=0, keepdims=True)
        ids = lax.broadcasted_iota(jnp.int32, logits.shape, 0) + c * chunk
        picked = picked + jnp.sum(jnp.where(ids == wanted, logits, 0.0), axis=0, keepdims=True)
        return new_top, total, picked

    start = (jnp.full((1, count), -1e30, F32), jnp.zeros((1, count), F32), jnp.zeros((1, count), F32))
    top, total, picked = lax.fori_loop(0, n_chunks, visit, start)
    stats[r] = jnp.concatenate([top, total, picked, jnp.zeros((5, count), F32)], axis=0)

    stat_copies = []
    for step in range(1, n_req):
        copy = remote(stats.at[r], stats.at[r], ss_sem.at[step], sr_sem.at[r], near(step))
        copy.start()
        stat_copies.append(copy)
    for step in range(1, n_req):
        source = lax.rem(r + n_req - step, n_req)
        remote(stats.at[source], stats.at[source], ss_sem.at[step], sr_sem.at[source], near(step)).wait_recv()
    every = stats[...]
    top = jnp.max(every[:, 0, :], axis=0, keepdims=True)
    total = jnp.sum(every[:, 1, :] * jnp.exp(every[:, 0, :] - top), axis=0, keepdims=True)
    picked = jnp.sum(every[:, 2, :], axis=0, keepdims=True)
    lpz[z] = jnp.broadcast_to(picked - top - jnp.log(total), (8, count))
    lp_copies = []
    for step in range(1, NTP):
        copy = remote(lpz.at[z], lpz.at[z], ls_sem.at[step], lr_sem.at[z], along(step))
        copy.start()
        lp_copies.append(copy)
    for step in range(1, n_req):
        source = lax.rem(r + n_req - step, n_req)
        remote(acc_all.at[source], acc_all.at[source], bs_sem.at[step], br_sem.at[source], near(step)).wait_recv()
    for i in range(slots):
        kept = jnp.zeros(acc_out.shape[1:], F32)
        for slot in range(n_req * slots):
            rows_of = acc_all[slot // slots, slot % slots * ACC : (slot % slots + 1) * ACC, :].astype(F32)
            kept = kept + jnp.where(deal_ref[slot] == r * slots + i, rows_of, 0.0)
        acc_out[i] = kept.astype(BF16)
    dealt = jnp.zeros((1, count), jnp.int32)
    for slot in range(n_req * slots):
        dealt = jnp.where(lane_slot == slot, deal_ref[slot], dealt)
    fold = lax.broadcasted_iota(jnp.int32, (count, tree), 0)
    node_id = lax.broadcasted_iota(jnp.int32, (count, tree), 1)
    fold = (lax.rem(fold, share) == lax.rem(node_id, share)).astype(F32)
    keep_z = lax.broadcasted_iota(jnp.int32, (NTP, tree), 0) == lax.broadcasted_iota(jnp.int32, (NTP, tree), 1) // share
    for step in range(1, NTP):
        source = lax.rem(z + NTP - step, NTP)
        remote(lpz.at[source], lpz.at[source], ls_sem.at[step], lr_sem.at[source], along(step)).wait_recv()
    by_z = lpz[:, 0, :]
    for i in range(slots):
        mine = jnp.where(dealt == r * slots + i, by_z, 0.0)
        folded = jnp.dot(mine, fold, precision=HIGH, preferred_element_type=F32)
        lp_out[i : i + 1, :] = jnp.sum(jnp.where(keep_z, folded, 0.0), axis=0, keepdims=True)

    for s, f in stages:
        far_copy(s, f).wait_send()
        mate_copy(s, f).wait_send()
        edge_copy(s, f).wait_send()
        for step in range(chips):
            gather_copy(s, f, r, gs_sem.at[s, f, step], sibling).wait_send()
        for step in range(1, chips):
            gather_copy(s, f, r, gf_sem.at[s, f, step], sibling).wait_send()
    for copy in acc_send + acc_copies + stat_copies + lp_copies + norm_copies:
        copy.wait_send()


def local(
    stream,
    queries,
    key_new,
    value_new,
    cache_key,
    cache_value,
    cache_length,
    parents,
    accept,
    out_weight,
    norm_gain,
    head_weight,
    candidate,
    dealing,
):
    slots, tree, width = queries.shape
    model = stream.shape[2]
    n_req = lax.axis_size("req")
    share = tree // NTP
    count = slots * n_req * share
    dslice = model // NTP
    chips = n_req // 2
    vocab = head_weight.shape[0]
    cache = cache_key.shape[1]
    vmem = pl.BlockSpec(memory_space=pltpu.VMEM)
    hbm = pl.BlockSpec(memory_space=pl.ANY)
    dma = pltpu.SemaphoreType.DMA
    features = len(feature_chunks(model))
    smem = pl.BlockSpec(memory_space=pltpu.SMEM)
    return pl.pallas_call(
        functools.partial(kernel, n_req),
        out_shape=(
            jax.ShapeDtypeStruct((slots, tree), F32),
            jax.ShapeDtypeStruct((slots, ACC, dslice), BF16),
        ),
        in_specs=[smem] + [vmem] * 4 + [smem] + [hbm] * 8,
        out_specs=(vmem, vmem),
        scratch_shapes=[
            pltpu.VMEM((slots, tree, width), BF16),
            pltpu.VMEM((slots, tree, width), BF16),
            pltpu.VMEM((slots, tree, width), BF16),
            pltpu.VMEM((slots, share, model), BF16),
            pltpu.VMEM((slots, cache, width), BF16),
            pltpu.VMEM((slots, cache, width), BF16),
            pltpu.VMEM((width, model), BF16),
            pltpu.VMEM((vocab, model), BF16),
            pltpu.VMEM((slots, tree, model), BF16),
            pltpu.VMEM((slots, 3, share, model), BF16),
            pltpu.VMEM((slots, share, model), BF16),
            pltpu.VMEM((slots, n_req, share, model), BF16),
            pltpu.VMEM((slots, share, model), BF16),
            pltpu.VMEM((vocab, count), F32),
            pltpu.VMEM((n_req, 8, count), F32),
            pltpu.VMEM((NTP, slots, ACC, dslice), F32),
            pltpu.VMEM((2 * NTP + 1, slots * ACC, dslice), BF16),
            pltpu.VMEM((n_req, slots * ACC, dslice), BF16),
            pltpu.VMEM((n_req, 8, count), F32),
            pltpu.VMEM((NTP, 8, count), F32),
            dma((9,)),
            dma((vocab // vocab_chunk(vocab),)),
            dma((slots, features, 3)),
            dma((slots, features, 3)),
            dma((slots, features, chips)),
            dma((slots, features, chips)),
            dma((slots, features, n_req)),
            dma((NTP,)),
            dma((NTP,)),
            dma((n_req,)),
            dma((n_req,)),
            dma((n_req,)),
            dma((n_req,)),
            dma((NTP,)),
            dma((NTP,)),
            dma((n_req,)),
            dma((n_req,)),
        ],
        compiler_params=pltpu.CompilerParams(
            collective_id=0, has_side_effects=True, vmem_limit_bytes=62 * 1024 * 1024
        ),
    )(
        cache_length,
        parents,
        accept,
        norm_gain,
        candidate,
        dealing,
        queries,
        key_new,
        value_new,
        stream,
        cache_key,
        cache_value,
        out_weight,
        head_weight,
    )


def solution(mesh):
    placed = (
        P("req", None, None),
        P("req", None, "tp"),
        P("req", None, "tp"),
        P("req", None, "tp"),
        P("req", None, "tp"),
        P("req", None, "tp"),
        P("req"),
        P("req", None),
        P("req", None, None),
        P("tp", None),
        P(),
        P("req", None),
        P(),
        P(),
    )
    return jax.shard_map(
        local,
        mesh=mesh,
        in_specs=placed,
        out_specs=(P("req", None), P("req", None, "tp")),
        check_vma=False,
    )
```

```python
import functools

import jax
import jax.numpy as jnp
from jax import lax
from jax.experimental import pallas as pl
from jax.experimental.pallas import tpu as pltpu
from jax.sharding import PartitionSpec as P

HD = 224
ACC = 8
EPS = 1e-05
NTP = 4
MESH = pl.DeviceIdType.MESH
NT = (((1,), (1,)), ((), ()))
HIGH = lax.Precision.HIGHEST
F32 = jnp.float32
BF16 = jnp.bfloat16


def feature_chunks(model):
    size = 1024
    return [(first, min(size, model - first)) for first in range(0, model, size)]


def vocab_chunk(vocab):
    for size in (2000, 512, 256):
        if vocab % size == 0:
            return size
    return vocab


def kernel(
    n_req,
    len_ref,
    par_ref,
    acc_ref,
    gain_ref,
    cand_ref,
    deal_ref,
    q_hbm,
    kn_hbm,
    vn_hbm,
    stream_hbm,
    ck_hbm,
    cv_hbm,
    ow_hbm,
    hw_hbm,
    lp_out,
    acc_out,
    q_v,
    kn_v,
    vn_v,
    st_v,
    ck_v,
    cv_v,
    ow_v,
    hw_v,
    part,
    zrecv,
    zfwd,
    gat,
    post_v,
    logits_v,
    norms,
    acc_part,
    acc_recv,
    acc_all,
    stats,
    lpz,
    in_sem,
    hw_sem,
    zs_sem,
    zr_sem,
    gs_sem,
    gf_sem,
    gr_sem,
    as_sem,
    ar_sem,
    bs_sem,
    br_sem,
    ss_sem,
    sr_sem,
    ls_sem,
    lr_sem,
    ns_sem,
    nr_sem,
):
    slots, tree, width = q_v.shape
    heads = width // HD
    model = ow_v.shape[1]
    vocab = hw_v.shape[0]
    share = tree // NTP
    rows = n_req * share
    dslice = model // NTP
    chips = n_req // 2
    r = lax.axis_index("req")
    z = lax.axis_index("tp")
    chip = r // 2
    core = r % 2
    sibling = chip * 2 + (1 - core)

    def near(step):
        return lax.rem(r + step, n_req), z

    def along(step):
        return r, lax.rem(z + step, NTP)

    loads = {}

    def load(name, index, src, dst):
        loads[name] = pltpu.make_async_copy(src, dst, in_sem.at[index])
        loads[name].start()

    load("q", 0, q_hbm, q_v)
    load("k0", 1, ck_hbm.at[0], ck_v.at[0])
    load("kn", 2, kn_hbm, kn_v)
    load("vn", 3, vn_hbm, vn_v)
    load("v0", 4, cv_hbm.at[0], cv_v.at[0])
    load("ow", 5, ow_hbm, ow_v)
    own_rows = pl.ds(pl.multiple_of(z * share, share), share)
    chunk = vocab_chunk(vocab)
    n_chunks = vocab // chunk
    head_loads = []
    for c in range(n_chunks):
        rows_c = pl.ds(c * chunk, chunk)
        head_loads.append(pltpu.make_async_copy(hw_hbm.at[rows_c, :], hw_v.at[rows_c, :], hw_sem.at[c]))

    barrier = pltpu.get_barrier_semaphore()
    for step in range(1, n_req):
        pl.semaphore_signal(barrier, inc=1, device_id=near(step), device_id_type=MESH)
    for step in range(1, NTP):
        pl.semaphore_signal(barrier, inc=1, device_id=along(step), device_id_type=MESH)

    def remote(src, dst, send, recv, device):
        return pltpu.make_async_remote_copy(
            src_ref=src, dst_ref=dst, send_sem=send, recv_sem=recv, device_id=device, device_id_type=MESH
        )

    row_id = lax.broadcasted_iota(jnp.int32, (tree, tree), 0)
    col_id = lax.broadcasted_iota(jnp.int32, (tree, tree), 1)
    eye = (row_id == col_id).astype(F32)
    visible = []
    for s in range(slots):
        step_t = (row_id == par_ref[s : s + 1, :]).astype(F32).astype(BF16)
        reached = eye
        for doubling in range((ACC - 1).bit_length()):
            reached = reached + lax.dot_general(reached.astype(BF16), step_t, NT, preferred_element_type=F32)
            step_t = jnp.dot(step_t, step_t, preferred_element_type=F32).astype(BF16)
        visible.append(reached)

    lane = lax.broadcasted_iota(jnp.int32, (tree, width), 1)
    head_mask = [(lane >= h * HD) & (lane < (h + 1) * HD) for h in range(heads)]
    scale = HD ** (-0.5)

    def attend(s):
        query = q_v[s]
        blocks = jnp.concatenate([jnp.where(m, query, jnp.zeros_like(query)) for m in head_mask], axis=0)
        past = lax.dot_general(blocks, ck_v[s], NT, preferred_element_type=F32) * scale
        fresh = lax.dot_general(blocks, kn_v[s], NT, preferred_element_type=F32) * scale
        position = lax.broadcasted_iota(jnp.int32, past.shape, 1)
        past = jnp.where(position < len_ref[s], past, -jnp.inf)
        seen = jnp.concatenate([visible[s]] * heads, axis=0)
        fresh = jnp.where(seen > 0.5, fresh, -jnp.inf)
        top = jnp.maximum(jnp.max(past, axis=1, keepdims=True), jnp.max(fresh, axis=1, keepdims=True))
        past = jnp.exp(past - top)
        fresh = jnp.exp(fresh - top)
        total = jnp.sum(past, axis=1, keepdims=True) + jnp.sum(fresh, axis=1, keepdims=True)
        if s == 0:
            loads["v0"].wait()
        else:
            loads["v1"].wait()
        mixed = jnp.dot(past.astype(BF16), cv_v[s], preferred_element_type=F32)
        mixed = mixed + jnp.dot(fresh.astype(BF16), vn_v[s], preferred_element_type=F32)
        mixed = mixed / total
        joined = jnp.zeros((tree, width), F32)
        for h in range(heads):
            joined = jnp.where(head_mask[h], mixed[h * tree : (h + 1) * tree, :], joined)
        return joined.astype(BF16)

    low = z < 2
    edge = (z == 0) | (z == 3)
    mate = z + 1 - 2 * (z % 2)
    far_edge = jnp.where(low, 3, 0)
    far_inner = jnp.where(low, 2, 1)

    def block(index):
        return pl.ds(pl.multiple_of(index * share, share), share)

    far_slot = jnp.where(edge, 2, 1)
    chunks = feature_chunks(model)
    n_feat = len(chunks)
    stages = [(s, f) for s in range(slots) for f in range(n_feat)]
    spans = [pl.ds(first, size) for first, size in chunks]

    def z_copy(s, f, src, slot, lane_sem, device):
        dst = zrecv.at[s, slot, :, spans[f]]
        return remote(src, dst, zs_sem.at[s, f, lane_sem], zr_sem.at[s, f, slot], (r, device))

    def far_copy(s, f):
        return z_copy(s, f, part.at[s, block(far_edge), spans[f]], far_slot, 0, far_edge)

    def mate_copy(s, f):
        return z_copy(s, f, part.at[s, block(mate), spans[f]], 0, 1, mate)

    def edge_copy(s, f):
        return z_copy(s, f, part.at[s, block(far_inner), spans[f]], 2, 2, mate)

    def sum_copy(s, f):
        return z_copy(s, f, zfwd.at[s, :, spans[f]], 1, 2, far_inner)

    def landed(s, f, slot):
        z_copy(s, f, zfwd.at[s, :, spans[f]], slot, 0, mate).wait_recv()

    loads["q"].wait()
    for s in range(slots):
        loads["k0" if s == 0 else "k1"].wait()
        if s == 0:
            loads["kn"].wait()
            loads["vn"].wait()
            load("k1", 6, ck_hbm.at[1], ck_v.at[1])
            load("v1", 7, cv_hbm.at[1], cv_v.at[1])
            load("st", 8, stream_hbm.at[:, own_rows, :], st_v)
        attention = attend(s)
        if s == 0:
            loads["ow"].wait()
            for copy in head_loads:
                copy.start()
            pl.semaphore_wait(barrier, n_req - 1 + NTP - 1)
        for f in range(n_feat):
            part[s, :, spans[f]] = jnp.dot(
                attention, ow_v[:, spans[f]], preferred_element_type=F32
            ).astype(BF16)

            @pl.when(edge)
            def _(s=s, f=f):
                edge_copy(s, f).start()

            far_copy(s, f).start()
            mate_copy(s, f).start()

    loads["st"].wait()

    def forward_sum(s, f):
        @pl.when(jnp.logical_not(edge))
        def _():
            landed(s, f, 2)
            own = part[s, block(far_inner), spans[f]].astype(F32)
            zfwd[s, :, spans[f]] = (own + zrecv[s, 2, :, spans[f]].astype(F32)).astype(BF16)
            sum_copy(s, f).start()

    gather_peers = [lax.rem(chip + step, chips) * 2 + core for step in range(1, chips)]
    gather_sources = [lax.rem(chip + chips - step, chips) * 2 + core for step in range(1, chips)]

    def gather_copy(s, f, owner, send, device):
        place = gat.at[s, owner, :, spans[f]]
        return remote(place, place, send, gr_sem.at[s, f, owner], (device, z))

    squares = [jnp.zeros((share, 1), F32) for s in range(slots)]

    def finish(s, f):
        landed(s, f, 0)
        landed(s, f, 1)

        @pl.when(edge)
        def _():
            landed(s, f, 2)

        span = spans[f]
        total = part[s, own_rows, span].astype(F32) + zrecv[s, 0, :, span].astype(F32)
        total = total + zrecv[s, 1, :, span].astype(F32)
        third = jnp.where(edge, zrecv[s, 2, :, span].astype(F32), 0.0)
        post = (st_v[s, :, span].astype(F32) + (total + third)).astype(BF16)
        post_v[s, :, span] = post
        post = post.astype(F32)
        squares[s] = squares[s] + jnp.sum(post * post, axis=1, keepdims=True)
        gat[s, r, :, span] = (post * gain_ref[span].reshape(1, chunks[f][1])).astype(BF16)
        for step in range(1, chips):
            gather_copy(s, f, r, gs_sem.at[s, f, step], gather_peers[step - 1]).start()
        gather_copy(s, f, r, gs_sem.at[s, f, 0], sibling).start()

    def forward_gather(s, f):
        for step in range(1, chips):
            source = gather_sources[step - 1]
            gather_copy(s, f, source, gf_sem.at[s, f, step], sibling).wait_recv()
            gather_copy(s, f, source, gf_sem.at[s, f, step], sibling).start()

    def gathered(s, f):
        gather_copy(s, f, sibling, gs_sem.at[s, f, 0], sibling).wait_recv()
        for step in range(1, chips):
            other = lax.rem(chip + step, chips) * 2 + (1 - core)
            gather_copy(s, f, other, gs_sem.at[s, f, 0], sibling).wait_recv()

    count = slots * rows

    def words_at(c):
        return pl.ds(pl.multiple_of(c * chunk, chunk), chunk)

    def head_part(f, c):
        inputs = gat[:, :, :, spans[f]].reshape(count, chunks[f][1])
        return lax.dot_general(hw_v[words_at(c), spans[f]], inputs, NT, preferred_element_type=F32)

    def score(f):
        for s in range(slots):
            gathered(s, f)
        if f == 0:
            for copy in head_loads:
                copy.wait()
        if f < n_feat - 1:

            def visit(c, carry):
                if f == 0:
                    logits_v[words_at(c), :] = head_part(f, c)
                else:
                    logits_v[words_at(c), :] += head_part(f, c)
                return carry

            lax.fori_loop(0, n_chunks, visit, 0)

    lane_id = lax.broadcasted_iota(jnp.int32, (1, count), 1)
    lane_slot = lax.rem(lane_id // share, n_req) * slots + lane_id // rows
    lane_node = lax.rem(lane_id, share)

    forward_sum(*stages[0])
    n_stage = len(stages)
    norm_copies = []
    for k in range(n_stage):
        if k + 1 < n_stage:
            forward_sum(*stages[k + 1])
        finish(*stages[k])
        if k == n_stage - 1:
            own_lane = [
                lax.broadcasted_iota(jnp.int32, (share, count), 1)
                == lax.broadcasted_iota(jnp.int32, (share, count), 0) + (s * rows + r * share)
                for s in range(slots)
            ]
            placed = sum(
                jnp.sum(jnp.where(own_lane[s], lax.rsqrt(squares[s] / model + EPS), 0.0), axis=0, keepdims=True)
                for s in range(slots)
            )
            norms[r] = jnp.broadcast_to(placed, (8, count))
            for step in range(1, n_req):
                copy = remote(norms.at[r], norms.at[r], ns_sem.at[step], nr_sem.at[r], near(step))
                copy.start()
                norm_copies.append(copy)
        if k >= 1:
            forward_gather(*stages[k - 1])
        if k >= n_feat + 2:
            score(k - n_feat - 2)
    forward_gather(*stages[n_stage - 1])

    node = lax.broadcasted_iota(jnp.int32, (tree, share), 0)
    place = lax.broadcasted_iota(jnp.int32, (tree, share), 1)
    pick = (node == place + z * share).astype(F32).astype(BF16)
    for s in range(slots):
        chosen = jnp.dot(acc_ref[s].astype(F32).astype(BF16), pick, preferred_element_type=F32).astype(BF16)
        for k in range(NTP):
            acc_part[k, s] = jnp.dot(
                chosen, post_v[s, :, k * dslice : (k + 1) * dslice], preferred_element_type=F32
            )
    acc_send = []
    for k in range(NTP):
        acc_recv[NTP + 1 + k] = jnp.concatenate([acc_part[k, s] for s in range(slots)], axis=0).astype(BF16)
    for step in range(1, NTP):
        target = lax.rem(z + step, NTP)
        copy = remote(
            acc_recv.at[NTP + 1 + target], acc_recv.at[step], as_sem.at[step], ar_sem.at[step], (r, target)
        )
        copy.start()
        acc_send.append(copy)

    wide = lax.broadcasted_iota(jnp.int32, (tree, count), 0)
    spread = (wide == lane_node + z * share).astype(F32)
    ids_by_slot = jnp.dot(cand_ref[...].astype(F32), spread, precision=HIGH, preferred_element_type=F32)
    slot_row = lax.broadcasted_iota(jnp.int32, ids_by_slot.shape, 0)
    wanted = jnp.sum(jnp.where(slot_row == lane_slot, ids_by_slot, 0.0), axis=0, keepdims=True)
    wanted = (wanted + 0.5).astype(jnp.int32) - r * vocab

    for f in range(max(n_feat - 2, 0), n_feat - 1):
        score(f)

    for copy in acc_send:
        copy.wait_recv()
    compact = acc_recv[NTP + 1 + z].astype(F32)
    for step in range(1, NTP):
        compact = compact + acc_recv[step].astype(F32)
    acc_all[r] = compact.astype(BF16)
    acc_copies = []
    for step in range(1, n_req):
        copy = remote(acc_all.at[r], acc_all.at[r], bs_sem.at[step], br_sem.at[r], near(step))
        copy.start()
        acc_copies.append(copy)

    score(n_feat - 1)
    for step in range(1, n_req):
        source = lax.rem(r + n_req - step, n_req)
        remote(norms.at[source], norms.at[source], ns_sem.at[step], nr_sem.at[source], near(step)).wait_recv()
    inverse = jnp.sum(norms[:, 0, :], axis=0, keepdims=True)

    def visit(c, carry):
        top, total, picked = carry
        logits = head_part(n_feat - 1, c)
        if n_feat > 1:
            logits = logits + logits_v[words_at(c), :]
        logits = logits * inverse
        new_top = jnp.maximum(top, jnp.max(logits, axis=0, keepdims=True))
        total = total * jnp.exp(top - new_top) + jnp.sum(jnp.exp(logits - new_top), axis=0, keepdims=True)
        ids = lax.broadcasted_iota(jnp.int32, logits.shape, 0) + c * chunk
        picked = picked + jnp.sum(jnp.where(ids == wanted, logits, 0.0), axis=0, keepdims=True)
        return new_top, total, picked

    start = (jnp.full((1, count), -1e30, F32), jnp.zeros((1, count), F32), jnp.zeros((1, count), F32))
    top, total, picked = lax.fori_loop(0, n_chunks, visit, start)
    stats[r] = jnp.concatenate([top, total, picked, jnp.zeros((5, count), F32)], axis=0)

    stat_copies = []
    for step in range(1, n_req):
        copy = remote(stats.at[r], stats.at[r], ss_sem.at[step], sr_sem.at[r], near(step))
        copy.start()
        stat_copies.append(copy)
    for s, f in stages:
        far_copy(s, f).wait_send()
        mate_copy(s, f).wait_send()
        edge_copy(s, f).wait_send()
        for step in range(chips):
            gather_copy(s, f, r, gs_sem.at[s, f, step], sibling).wait_send()
        for step in range(1, chips):
            gather_copy(s, f, r, gf_sem.at[s, f, step], sibling).wait_send()
    for copy in acc_send + acc_copies + norm_copies:
        copy.wait_send()
    for step in range(1, n_req):
        source = lax.rem(r + n_req - step, n_req)
        remote(stats.at[source], stats.at[source], ss_sem.at[step], sr_sem.at[source], near(step)).wait_recv()
    every = stats[...]
    top = jnp.max(every[:, 0, :], axis=0, keepdims=True)
    total = jnp.sum(every[:, 1, :] * jnp.exp(every[:, 0, :] - top), axis=0, keepdims=True)
    picked = jnp.sum(every[:, 2, :], axis=0, keepdims=True)
    lpz[z] = jnp.concatenate([picked - top, -jnp.log(total), jnp.zeros((6, count), F32)], axis=0)
    lp_copies = []
    for step in range(1, NTP):
        copy = remote(lpz.at[z], lpz.at[z], ls_sem.at[step], lr_sem.at[z], along(step))
        copy.start()
        lp_copies.append(copy)
    for step in range(1, n_req):
        source = lax.rem(r + n_req - step, n_req)
        remote(acc_all.at[source], acc_all.at[source], bs_sem.at[step], br_sem.at[source], near(step)).wait_recv()
    for i in range(slots):
        kept = jnp.zeros(acc_out.shape[1:], F32)
        for slot in range(n_req * slots):
            rows_of = acc_all[slot // slots, slot % slots * ACC : (slot % slots + 1) * ACC, :].astype(F32)
            kept = kept + jnp.where(deal_ref[slot] == r * slots + i, rows_of, 0.0)
        acc_out[i] = kept
    dealt = jnp.zeros((1, count), jnp.int32)
    for slot in range(n_req * slots):
        dealt = jnp.where(lane_slot == slot, deal_ref[slot], dealt)
    fold = lax.broadcasted_iota(jnp.int32, (count, tree), 0)
    node_id = lax.broadcasted_iota(jnp.int32, (count, tree), 1)
    fold = (lax.rem(fold, share) == lax.rem(node_id, share)).astype(F32)
    keep_z = lax.broadcasted_iota(jnp.int32, (NTP, tree), 0) == lax.broadcasted_iota(jnp.int32, (NTP, tree), 1) // share
    for step in range(1, NTP):
        source = lax.rem(z + NTP - step, NTP)
        remote(lpz.at[source], lpz.at[source], ls_sem.at[step], lr_sem.at[source], along(step)).wait_recv()
    for i in range(slots):
        for term in range(2):
            mine = jnp.where(dealt == r * slots + i, lpz[:, term, :], 0.0)
            folded = jnp.dot(mine, fold, precision=HIGH, preferred_element_type=F32)
            lp_out[term, i : i + 1, :] = jnp.sum(jnp.where(keep_z, folded, 0.0), axis=0, keepdims=True)

    for copy in stat_copies + lp_copies:
        copy.wait_send()


def local(
    stream,
    queries,
    key_new,
    value_new,
    cache_key,
    cache_value,
    cache_length,
    parents,
    accept,
    out_weight,
    norm_gain,
    head_weight,
    candidate,
    dealing,
):
    slots, tree, width = queries.shape
    model = stream.shape[2]
    n_req = lax.axis_size("req")
    share = tree // NTP
    count = slots * n_req * share
    dslice = model // NTP
    chips = n_req // 2
    vocab = head_weight.shape[0]
    cache = cache_key.shape[1]
    vmem = pl.BlockSpec(memory_space=pltpu.VMEM)
    hbm = pl.BlockSpec(memory_space=pl.ANY)
    dma = pltpu.SemaphoreType.DMA
    features = len(feature_chunks(model))
    smem = pl.BlockSpec(memory_space=pltpu.SMEM)
    terms, states = pl.pallas_call(
        functools.partial(kernel, n_req),
        out_shape=(
            jax.ShapeDtypeStruct((2, slots, tree), F32),
            jax.ShapeDtypeStruct((slots, ACC, dslice), F32),
        ),
        in_specs=[smem] + [vmem] * 4 + [smem] + [hbm] * 8,
        out_specs=(vmem, vmem),
        scratch_shapes=[
            pltpu.VMEM((slots, tree, width), BF16),
            pltpu.VMEM((slots, tree, width), BF16),
            pltpu.VMEM((slots, tree, width), BF16),
            pltpu.VMEM((slots, share, model), BF16),
            pltpu.VMEM((slots, cache, width), BF16),
            pltpu.VMEM((slots, cache, width), BF16),
            pltpu.VMEM((width, model), BF16),
            pltpu.VMEM((vocab, model), BF16),
            pltpu.VMEM((slots, tree, model), BF16),
            pltpu.VMEM((slots, 3, share, model), BF16),
            pltpu.VMEM((slots, share, model), BF16),
            pltpu.VMEM((slots, n_req, share, model), BF16),
            pltpu.VMEM((slots, share, model), BF16),
            pltpu.VMEM((vocab, count), F32),
            pltpu.VMEM((n_req, 8, count), F32),
            pltpu.VMEM((NTP, slots, ACC, dslice), F32),
            pltpu.VMEM((2 * NTP + 1, slots * ACC, dslice), BF16),
            pltpu.VMEM((n_req, slots * ACC, dslice), BF16),
            pltpu.VMEM((n_req, 8, count), F32),
            pltpu.VMEM((NTP, 8, count), F32),
            dma((9,)),
            dma((vocab // vocab_chunk(vocab),)),
            dma((slots, features, 3)),
            dma((slots, features, 3)),
            dma((slots, features, chips)),
            dma((slots, features, chips)),
            dma((slots, features, n_req)),
            dma((NTP,)),
            dma((NTP,)),
            dma((n_req,)),
            dma((n_req,)),
            dma((n_req,)),
            dma((n_req,)),
            dma((NTP,)),
            dma((NTP,)),
            dma((n_req,)),
            dma((n_req,)),
        ],
        compiler_params=pltpu.CompilerParams(
            collective_id=0, has_side_effects=True, vmem_limit_bytes=62 * 1024 * 1024
        ),
    )(
        cache_length,
        parents,
        accept,
        norm_gain,
        candidate,
        dealing,
        queries,
        key_new,
        value_new,
        stream,
        cache_key,
        cache_value,
        out_weight,
        head_weight,
    )
    return (terms[0] + terms[1], states.astype(BF16))


def solution(mesh):
    placed = (
        P("req", None, None),
        P("req", None, "tp"),
        P("req", None, "tp"),
        P("req", None, "tp"),
        P("req", None, "tp"),
        P("req", None, "tp"),
        P("req"),
        P("req", None),
        P("req", None, None),
        P("tp", None),
        P(),
        P("req", None),
        P(),
        P(),
    )
    return jax.shard_map(
        local,
        mesh=mesh,
        in_specs=placed,
        out_specs=(P("req", None), P("req", None, "tp")),
        check_vma=False,
    )
```

```python
import functools

import jax
import jax.numpy as jnp
from jax import lax
from jax.experimental import pallas as pl
from jax.experimental.pallas import tpu as pltpu
from jax.sharding import PartitionSpec as P

HD = 224
ACC = 8
EPS = 1e-05
NTP = 4
MESH = pl.DeviceIdType.MESH
NT = (((1,), (1,)), ((), ()))
HIGH = lax.Precision.HIGHEST
F32 = jnp.float32
BF16 = jnp.bfloat16


def feature_chunks(model):
    size = 1024
    return [(first, min(size, model - first)) for first in range(0, model, size)]


def vocab_chunk(vocab):
    for size in (2000, 512, 256):
        if vocab % size == 0:
            return size
    return vocab


def kernel(
    n_req,
    len_ref,
    par_ref,
    acc_ref,
    gain_ref,
    cand_ref,
    deal_ref,
    q_hbm,
    kn_hbm,
    vn_hbm,
    stream_hbm,
    ck_hbm,
    cv_hbm,
    ow_hbm,
    hw_hbm,
    lp_out,
    acc_out,
    q_v,
    kn_v,
    vn_v,
    st_v,
    ck_v,
    cv_v,
    ow_v,
    hw_v,
    part,
    zrecv,
    zfwd,
    gat,
    post_v,
    logits_v,
    norms,
    acc_part,
    acc_recv,
    acc_all,
    stats,
    lpz,
    in_sem,
    hw_sem,
    zs_sem,
    zr_sem,
    gs_sem,
    gf_sem,
    gr_sem,
    as_sem,
    ar_sem,
    bs_sem,
    br_sem,
    ss_sem,
    sr_sem,
    ls_sem,
    lr_sem,
    ns_sem,
    nr_sem,
):
    slots, tree, width = q_v.shape
    heads = width // HD
    model = ow_v.shape[1]
    vocab = hw_v.shape[0]
    share = tree // NTP
    rows = n_req * share
    dslice = model // NTP
    chips = n_req // 2
    r = lax.axis_index("req")
    z = lax.axis_index("tp")
    chip = r // 2
    core = r % 2
    sibling = chip * 2 + (1 - core)

    def near(step):
        return lax.rem(r + step, n_req), z

    def along(step):
        return r, lax.rem(z + step, NTP)

    loads = {}

    def load(name, index, src, dst):
        loads[name] = pltpu.make_async_copy(src, dst, in_sem.at[index])
        loads[name].start()

    load("q", 0, q_hbm, q_v)
    load("k0", 1, ck_hbm.at[0], ck_v.at[0])
    load("kn", 2, kn_hbm, kn_v)
    load("vn", 3, vn_hbm, vn_v)
    load("v0", 4, cv_hbm.at[0], cv_v.at[0])
    load("ow", 5, ow_hbm, ow_v)
    own_rows = pl.ds(pl.multiple_of(z * share, share), share)
    chunk = vocab_chunk(vocab)
    n_chunks = vocab // chunk
    head_loads = []
    for c in range(n_chunks):
        rows_c = pl.ds(c * chunk, chunk)
        head_loads.append(pltpu.make_async_copy(hw_hbm.at[rows_c, :], hw_v.at[rows_c, :], hw_sem.at[c]))

    barrier = pltpu.get_barrier_semaphore()
    for step in range(1, n_req):
        pl.semaphore_signal(barrier, inc=1, device_id=near(step), device_id_type=MESH)
    for step in range(1, NTP):
        pl.semaphore_signal(barrier, inc=1, device_id=along(step), device_id_type=MESH)

    def remote(src, dst, send, recv, device):
        return pltpu.make_async_remote_copy(
            src_ref=src, dst_ref=dst, send_sem=send, recv_sem=recv, device_id=device, device_id_type=MESH
        )

    row_id = lax.broadcasted_iota(jnp.int32, (tree, tree), 0)
    col_id = lax.broadcasted_iota(jnp.int32, (tree, tree), 1)
    eye = (row_id == col_id).astype(F32)
    visible = []
    for s in range(slots):
        step_t = (row_id == par_ref[s : s + 1, :]).astype(F32).astype(BF16)
        reached = eye
        for doubling in range((ACC - 1).bit_length()):
            reached = reached + lax.dot_general(reached.astype(BF16), step_t, NT, preferred_element_type=F32)
            step_t = jnp.dot(step_t, step_t, preferred_element_type=F32).astype(BF16)
        visible.append(reached)

    lane = lax.broadcasted_iota(jnp.int32, (tree, width), 1)
    head_mask = [(lane >= h * HD) & (lane < (h + 1) * HD) for h in range(heads)]
    scale = HD ** (-0.5)

    def attend(s):
        query = q_v[s]
        blocks = jnp.concatenate([jnp.where(m, query, jnp.zeros_like(query)) for m in head_mask], axis=0)
        past = lax.dot_general(blocks, ck_v[s], NT, preferred_element_type=F32) * scale
        fresh = lax.dot_general(blocks, kn_v[s], NT, preferred_element_type=F32) * scale
        position = lax.broadcasted_iota(jnp.int32, past.shape, 1)
        past = jnp.where(position < len_ref[s], past, -jnp.inf)
        seen = jnp.concatenate([visible[s]] * heads, axis=0)
        fresh = jnp.where(seen > 0.5, fresh, -jnp.inf)
        top = jnp.maximum(jnp.max(past, axis=1, keepdims=True), jnp.max(fresh, axis=1, keepdims=True))
        past = jnp.exp(past - top)
        fresh = jnp.exp(fresh - top)
        total = jnp.sum(past, axis=1, keepdims=True) + jnp.sum(fresh, axis=1, keepdims=True)
        if s == 0:
            loads["v0"].wait()
        else:
            loads["v1"].wait()
        mixed = jnp.dot(past.astype(BF16), cv_v[s], preferred_element_type=F32)
        mixed = mixed + jnp.dot(fresh.astype(BF16), vn_v[s], preferred_element_type=F32)
        mixed = mixed / total
        joined = jnp.zeros((tree, width), F32)
        for h in range(heads):
            joined = jnp.where(head_mask[h], mixed[h * tree : (h + 1) * tree, :], joined)
        return joined.astype(BF16)

    low = z < 2
    edge = (z == 0) | (z == 3)
    mate = z + 1 - 2 * (z % 2)
    far_edge = jnp.where(low, 3, 0)
    far_inner = jnp.where(low, 2, 1)

    def block(index):
        return pl.ds(pl.multiple_of(index * share, share), share)

    far_slot = jnp.where(edge, 2, 1)
    chunks = feature_chunks(model)
    n_feat = len(chunks)
    stages = [(s, f) for s in range(slots) for f in range(n_feat)]
    spans = [pl.ds(first, size) for first, size in chunks]

    def z_copy(s, f, src, slot, lane_sem, device):
        dst = zrecv.at[s, slot, :, spans[f]]
        return remote(src, dst, zs_sem.at[s, f, lane_sem], zr_sem.at[s, f, slot], (r, device))

    def far_copy(s, f):
        return z_copy(s, f, part.at[s, block(far_edge), spans[f]], far_slot, 0, far_edge)

    def mate_copy(s, f):
        return z_copy(s, f, part.at[s, block(mate), spans[f]], 0, 1, mate)

    def edge_copy(s, f):
        return z_copy(s, f, part.at[s, block(far_inner), spans[f]], 2, 2, mate)

    def sum_copy(s, f):
        return z_copy(s, f, zfwd.at[s, :, spans[f]], 1, 2, far_inner)

    def landed(s, f, slot):
        z_copy(s, f, zfwd.at[s, :, spans[f]], slot, 0, mate).wait_recv()

    def forward_sum(s, f):
        @pl.when(jnp.logical_not(edge))
        def _():
            landed(s, f, 2)
            own = part[s, block(far_inner), spans[f]].astype(F32)
            zfwd[s, :, spans[f]] = (own + zrecv[s, 2, :, spans[f]].astype(F32)).astype(BF16)
            sum_copy(s, f).start()

    loads["q"].wait()
    for s in range(slots):
        loads["k0" if s == 0 else "k1"].wait()
        if s == 0:
            loads["kn"].wait()
            loads["vn"].wait()
            load("k1", 6, ck_hbm.at[1], ck_v.at[1])
            load("v1", 7, cv_hbm.at[1], cv_v.at[1])
            load("st", 8, stream_hbm.at[:, own_rows, :], st_v)
        attention = attend(s)
        if s == 1:
            for f in range(n_feat):
                forward_sum(0, f)
        if s == 0:
            loads["ow"].wait()
            for copy in head_loads:
                copy.start()
            pl.semaphore_wait(barrier, n_req - 1 + NTP - 1)
        for f in range(n_feat):
            part[s, :, spans[f]] = jnp.dot(
                attention, ow_v[:, spans[f]], preferred_element_type=F32
            ).astype(BF16)

            @pl.when(edge)
            def _(s=s, f=f):
                edge_copy(s, f).start()

            far_copy(s, f).start()
            mate_copy(s, f).start()

    loads["st"].wait()

    gather_peers = [lax.rem(chip + step, chips) * 2 + core for step in range(1, chips)]
    gather_sources = [lax.rem(chip + chips - step, chips) * 2 + core for step in range(1, chips)]

    def gather_copy(s, f, owner, send, device):
        place = gat.at[s, owner, :, spans[f]]
        return remote(place, place, send, gr_sem.at[s, f, owner], (device, z))

    squares = [jnp.zeros((share, 1), F32) for s in range(slots)]

    def finish(s, f):
        landed(s, f, 0)
        landed(s, f, 1)

        @pl.when(edge)
        def _():
            landed(s, f, 2)

        span = spans[f]
        total = part[s, own_rows, span].astype(F32) + zrecv[s, 0, :, span].astype(F32)
        total = total + zrecv[s, 1, :, span].astype(F32)
        third = jnp.where(edge, zrecv[s, 2, :, span].astype(F32), 0.0)
        post = (st_v[s, :, span].astype(F32) + (total + third)).astype(BF16)
        post_v[s, :, span] = post
        post = post.astype(F32)
        squares[s] = squares[s] + jnp.sum(post * post, axis=1, keepdims=True)
        gat[s, r, :, span] = (post * gain_ref[span].reshape(1, chunks[f][1])).astype(BF16)
        for step in range(1, chips):
            gather_copy(s, f, r, gs_sem.at[s, f, step], gather_peers[step - 1]).start()
        gather_copy(s, f, r, gs_sem.at[s, f, 0], sibling).start()

    def forward_gather(s, f):
        for step in range(1, chips):
            source = gather_sources[step - 1]
            gather_copy(s, f, source, gf_sem.at[s, f, step], sibling).wait_recv()
            gather_copy(s, f, source, gf_sem.at[s, f, step], sibling).start()

    def gathered(s, f):
        gather_copy(s, f, sibling, gs_sem.at[s, f, 0], sibling).wait_recv()
        for step in range(1, chips):
            other = lax.rem(chip + step, chips) * 2 + (1 - core)
            gather_copy(s, f, other, gs_sem.at[s, f, 0], sibling).wait_recv()

    count = slots * rows

    def words_at(c):
        return pl.ds(pl.multiple_of(c * chunk, chunk), chunk)

    def head_part(f, c):
        inputs = gat[:, :, :, spans[f]].reshape(count, chunks[f][1])
        return lax.dot_general(hw_v[words_at(c), spans[f]], inputs, NT, preferred_element_type=F32)

    def score(f):
        for s in range(slots):
            gathered(s, f)
        if f == 0:
            for copy in head_loads:
                copy.wait()
        if f < n_feat - 1:

            def visit(c, carry):
                if f == 0:
                    logits_v[words_at(c), :] = head_part(f, c)
                else:
                    logits_v[words_at(c), :] += head_part(f, c)
                return carry

            lax.fori_loop(0, n_chunks, visit, 0)

    lane_id = lax.broadcasted_iota(jnp.int32, (1, count), 1)
    lane_slot = lax.rem(lane_id // share, n_req) * slots + lane_id // rows
    lane_node = lax.rem(lane_id, share)

    n_stage = len(stages)
    norm_copies = []
    for k in range(n_stage):
        if n_feat <= k + 1 < n_stage:
            forward_sum(*stages[k + 1])
        finish(*stages[k])
        if k == n_stage - 1:
            own_lane = [
                lax.broadcasted_iota(jnp.int32, (share, count), 1)
                == lax.broadcasted_iota(jnp.int32, (share, count), 0) + (s * rows + r * share)
                for s in range(slots)
            ]
            placed = sum(
                jnp.sum(jnp.where(own_lane[s], lax.rsqrt(squares[s] / model + EPS), 0.0), axis=0, keepdims=True)
                for s in range(slots)
            )
            norms[r] = jnp.broadcast_to(placed, (8, count))
            for step in range(1, n_req):
                copy = remote(norms.at[r], norms.at[r], ns_sem.at[step], nr_sem.at[r], near(step))
                copy.start()
                norm_copies.append(copy)
        if k >= 1:
            forward_gather(*stages[k - 1])
        if k >= n_feat + 2:
            score(k - n_feat - 2)
    forward_gather(*stages[n_stage - 1])

    node = lax.broadcasted_iota(jnp.int32, (tree, share), 0)
    place = lax.broadcasted_iota(jnp.int32, (tree, share), 1)
    pick = (node == place + z * share).astype(F32).astype(BF16)
    for s in range(slots):
        chosen = jnp.dot(acc_ref[s].astype(F32).astype(BF16), pick, preferred_element_type=F32).astype(BF16)
        for k in range(NTP):
            acc_part[k, s] = jnp.dot(
                chosen, post_v[s, :, k * dslice : (k + 1) * dslice], preferred_element_type=F32
            )
    acc_send = []
    for k in range(NTP):
        acc_recv[NTP + 1 + k] = jnp.concatenate([acc_part[k, s] for s in range(slots)], axis=0).astype(BF16)
    for step in range(1, NTP):
        target = lax.rem(z + step, NTP)
        copy = remote(
            acc_recv.at[NTP + 1 + target], acc_recv.at[step], as_sem.at[step], ar_sem.at[step], (r, target)
        )
        copy.start()
        acc_send.append(copy)

    wide = lax.broadcasted_iota(jnp.int32, (tree, count), 0)
    spread = (wide == lane_node + z * share).astype(F32)
    ids_by_slot = jnp.dot(cand_ref[...].astype(F32), spread, precision=HIGH, preferred_element_type=F32)
    slot_row = lax.broadcasted_iota(jnp.int32, ids_by_slot.shape, 0)
    wanted = jnp.sum(jnp.where(slot_row == lane_slot, ids_by_slot, 0.0), axis=0, keepdims=True)
    wanted = (wanted + 0.5).astype(jnp.int32) - r * vocab

    for f in range(max(n_feat - 2, 0), n_feat - 1):
        score(f)

    for copy in acc_send:
        copy.wait_recv()
    compact = acc_recv[NTP + 1 + z].astype(F32)
    for step in range(1, NTP):
        compact = compact + acc_recv[step].astype(F32)
    acc_all[r] = compact.astype(BF16)
    acc_copies = []
    for step in range(1, n_req):
        copy = remote(acc_all.at[r], acc_all.at[r], bs_sem.at[step], br_sem.at[r], near(step))
        copy.start()
        acc_copies.append(copy)

    score(n_feat - 1)
    for step in range(1, n_req):
        source = lax.rem(r + n_req - step, n_req)
        remote(norms.at[source], norms.at[source], ns_sem.at[step], nr_sem.at[source], near(step)).wait_recv()
    inverse = jnp.sum(norms[:, 0, :], axis=0, keepdims=True)

    def visit(c, carry):
        top, total, picked = carry
        logits = head_part(n_feat - 1, c)
        if n_feat > 1:
            logits = logits + logits_v[words_at(c), :]
        logits = logits * inverse
        new_top = jnp.maximum(top, jnp.max(logits, axis=0, keepdims=True))
        total = total * jnp.exp(top - new_top) + jnp.sum(jnp.exp(logits - new_top), axis=0, keepdims=True)
        ids = lax.broadcasted_iota(jnp.int32, logits.shape, 0) + c * chunk
        picked = picked + jnp.sum(jnp.where(ids == wanted, logits, 0.0), axis=0, keepdims=True)
        return new_top, total, picked

    start = (jnp.full((1, count), -1e30, F32), jnp.zeros((1, count), F32), jnp.zeros((1, count), F32))
    top, total, picked = lax.fori_loop(0, n_chunks, visit, start)
    stats[r] = jnp.concatenate([top, total, picked, jnp.zeros((5, count), F32)], axis=0)

    stat_copies = []
    for step in range(1, n_req):
        copy = remote(stats.at[r], stats.at[r], ss_sem.at[step], sr_sem.at[r], near(step))
        copy.start()
        stat_copies.append(copy)
    for s, f in stages:
        far_copy(s, f).wait_send()
        mate_copy(s, f).wait_send()
        edge_copy(s, f).wait_send()
        for step in range(chips):
            gather_copy(s, f, r, gs_sem.at[s, f, step], sibling).wait_send()
        for step in range(1, chips):
            gather_copy(s, f, r, gf_sem.at[s, f, step], sibling).wait_send()
    for copy in acc_send + acc_copies + norm_copies:
        copy.wait_send()
    for step in range(1, n_req):
        source = lax.rem(r + n_req - step, n_req)
        remote(stats.at[source], stats.at[source], ss_sem.at[step], sr_sem.at[source], near(step)).wait_recv()
    every = stats[...]
    top = jnp.max(every[:, 0, :], axis=0, keepdims=True)
    total = jnp.sum(every[:, 1, :] * jnp.exp(every[:, 0, :] - top), axis=0, keepdims=True)
    picked = jnp.sum(every[:, 2, :], axis=0, keepdims=True)
    lpz[z] = jnp.concatenate([picked - top, -jnp.log(total), jnp.zeros((6, count), F32)], axis=0)
    lp_copies = []
    for step in range(1, NTP):
        copy = remote(lpz.at[z], lpz.at[z], ls_sem.at[step], lr_sem.at[z], along(step))
        copy.start()
        lp_copies.append(copy)
    for step in range(1, n_req):
        source = lax.rem(r + n_req - step, n_req)
        remote(acc_all.at[source], acc_all.at[source], bs_sem.at[step], br_sem.at[source], near(step)).wait_recv()
    for i in range(slots):
        kept = jnp.zeros(acc_out.shape[1:], F32)
        for slot in range(n_req * slots):
            rows_of = acc_all[slot // slots, slot % slots * ACC : (slot % slots + 1) * ACC, :].astype(F32)
            kept = kept + jnp.where(deal_ref[slot] == r * slots + i, rows_of, 0.0)
        acc_out[i] = kept
    dealt = jnp.zeros((1, count), jnp.int32)
    for slot in range(n_req * slots):
        dealt = jnp.where(lane_slot == slot, deal_ref[slot], dealt)
    fold = lax.broadcasted_iota(jnp.int32, (count, tree), 0)
    node_id = lax.broadcasted_iota(jnp.int32, (count, tree), 1)
    fold = (lax.rem(fold, share) == lax.rem(node_id, share)).astype(F32)
    keep_z = lax.broadcasted_iota(jnp.int32, (NTP, tree), 0) == lax.broadcasted_iota(jnp.int32, (NTP, tree), 1) // share
    for step in range(1, NTP):
        source = lax.rem(z + NTP - step, NTP)
        remote(lpz.at[source], lpz.at[source], ls_sem.at[step], lr_sem.at[source], along(step)).wait_recv()
    for i in range(slots):
        for term in range(2):
            mine = jnp.where(dealt == r * slots + i, lpz[:, term, :], 0.0)
            folded = jnp.dot(mine, fold, precision=HIGH, preferred_element_type=F32)
            lp_out[term, i : i + 1, :] = jnp.sum(jnp.where(keep_z, folded, 0.0), axis=0, keepdims=True)

    for copy in stat_copies + lp_copies:
        copy.wait_send()


def local(
    stream,
    queries,
    key_new,
    value_new,
    cache_key,
    cache_value,
    cache_length,
    parents,
    accept,
    out_weight,
    norm_gain,
    head_weight,
    candidate,
    dealing,
):
    slots, tree, width = queries.shape
    model = stream.shape[2]
    n_req = lax.axis_size("req")
    share = tree // NTP
    count = slots * n_req * share
    dslice = model // NTP
    chips = n_req // 2
    vocab = head_weight.shape[0]
    cache = cache_key.shape[1]
    vmem = pl.BlockSpec(memory_space=pltpu.VMEM)
    hbm = pl.BlockSpec(memory_space=pl.ANY)
    dma = pltpu.SemaphoreType.DMA
    features = len(feature_chunks(model))
    smem = pl.BlockSpec(memory_space=pltpu.SMEM)
    terms, states = pl.pallas_call(
        functools.partial(kernel, n_req),
        out_shape=(
            jax.ShapeDtypeStruct((2, slots, tree), F32),
            jax.ShapeDtypeStruct((slots, ACC, dslice), F32),
        ),
        in_specs=[smem] + [vmem] * 4 + [smem] + [hbm] * 8,
        out_specs=(vmem, vmem),
        scratch_shapes=[
            pltpu.VMEM((slots, tree, width), BF16),
            pltpu.VMEM((slots, tree, width), BF16),
            pltpu.VMEM((slots, tree, width), BF16),
            pltpu.VMEM((slots, share, model), BF16),
            pltpu.VMEM((slots, cache, width), BF16),
            pltpu.VMEM((slots, cache, width), BF16),
            pltpu.VMEM((width, model), BF16),
            pltpu.VMEM((vocab, model), BF16),
            pltpu.VMEM((slots, tree, model), BF16),
            pltpu.VMEM((slots, 3, share, model), BF16),
            pltpu.VMEM((slots, share, model), BF16),
            pltpu.VMEM((slots, n_req, share, model), BF16),
            pltpu.VMEM((slots, share, model), BF16),
            pltpu.VMEM((vocab, count), F32),
            pltpu.VMEM((n_req, 8, count), F32),
            pltpu.VMEM((NTP, slots, ACC, dslice), F32),
            pltpu.VMEM((2 * NTP + 1, slots * ACC, dslice), BF16),
            pltpu.VMEM((n_req, slots * ACC, dslice), BF16),
            pltpu.VMEM((n_req, 8, count), F32),
            pltpu.VMEM((NTP, 8, count), F32),
            dma((9,)),
            dma((vocab // vocab_chunk(vocab),)),
            dma((slots, features, 3)),
            dma((slots, features, 3)),
            dma((slots, features, chips)),
            dma((slots, features, chips)),
            dma((slots, features, n_req)),
            dma((NTP,)),
            dma((NTP,)),
            dma((n_req,)),
            dma((n_req,)),
            dma((n_req,)),
            dma((n_req,)),
            dma((NTP,)),
            dma((NTP,)),
            dma((n_req,)),
            dma((n_req,)),
        ],
        compiler_params=pltpu.CompilerParams(
            collective_id=0, has_side_effects=True, vmem_limit_bytes=62 * 1024 * 1024
        ),
    )(
        cache_length,
        parents,
        accept,
        norm_gain,
        candidate,
        dealing,
        queries,
        key_new,
        value_new,
        stream,
        cache_key,
        cache_value,
        out_weight,
        head_weight,
    )
    return (terms[0] + terms[1], states.astype(BF16))


def solution(mesh):
    placed = (
        P("req", None, None),
        P("req", None, "tp"),
        P("req", None, "tp"),
        P("req", None, "tp"),
        P("req", None, "tp"),
        P("req", None, "tp"),
        P("req"),
        P("req", None),
        P("req", None, None),
        P("tp", None),
        P(),
        P("req", None),
        P(),
        P(),
    )
    return jax.shard_map(
        local,
        mesh=mesh,
        in_specs=placed,
        out_specs=(P("req", None), P("req", None, "tp")),
        check_vma=False,
    )
```
